512 devices in a mesh: src: 64 (over z, y), tgt: 8 (over x, core).
Axes of the slice: x: 4, y: 8, z: 8, core: 2. Of those that a mesh axis runs over, the one named last changes fastest.
Arguments:
- source_points: float32 [50, 131072], P(None, ('src', 'tgt')), may hold values from -1.8 to 1.8
- source_potential: float32 [131072], P(('src', 'tgt')), may hold values from -4 to 452
- source_logw: float32 [131072], P('src'), may hold values from -2 to 2
- target_points: float32 [50, 131072], P(None, 'tgt'), may hold values from -1.8 to 1.8
- target_logw: float32 [131072], P('tgt'), may hold values from -4 to 452
- pair_source: int32 [64, 8, 256], P('src', 'tgt'), may hold values from 0 to 15, as said below
- pair_target: int32 [64, 8, 256], P('src', 'tgt'), may hold values from 0 to 127
- pair_count: int32 [64, 8], P('src', 'tgt'), may hold values from 128 to 256, as said below
Outputs:
- target_potential: float32 [131072], P('tgt')
- updated_source: float32 [131072], P('src')
The draws below stay inside these ranges and needn't reach their ends.
Inputs may be any that keep to these rules, and one draw needn't show every extreme that they name: `pair_source`: on each device the pairs in the used slots are distinct; slots 0 to 127 are always used, name every target block of the device exactly once and every source block of the device at least once; unused slots hold numbers in range but are not pairs. `pair_count`: in every draw some device uses all 256 slots and another exactly 128.
All inputs are finite; a program needn't handle non-finite values.
Results may differ from the reference program's by a relative error of at most 0.0003.
Values sent between devices are 32-bit elements; how exact they have to be, the bound alone decides.
A program may use at most 64 MiB of HBM per device.

```python
import jax
import jax.numpy as jnp
from jax import lax

PC = 50
BLOCK = 128
SB_DEV = 16
TB_DEV = 128
PAIRS = 256
NS = 131072
NT = 131072
N_SRC = 64
N_TGT = 8


def draw_source_potential(key, part):
    key = jax.random.fold_in(key, 11)
    first = jax.random.fold_in(key, 0)
    return jnp.clip(jax.random.normal(first, (NS,), jnp.float32), -4.0, 4.0)


def draw_target_logw(key, part):
    key = jax.random.fold_in(key, 12)
    first = jax.random.fold_in(key, 0)
    base = jax.random.uniform(first, (NT,), jnp.float32, -2.0, 2.0)
    return base


def pair_tables(key):
    devices_all = N_SRC * N_TGT
    keys = jax.random.split(key, 7)
    tperm = jax.vmap(lambda k: jax.random.permutation(k, TB_DEV))(jax.random.split(keys[0], devices_all)).astype(jnp.int32)
    sperm = jax.vmap(lambda k: jax.random.permutation(k, SB_DEV))(jax.random.split(keys[1], devices_all)).astype(jnp.int32)
    extra_t = jax.vmap(lambda k: jax.random.permutation(k, TB_DEV))(jax.random.split(keys[2], devices_all)).astype(jnp.int32)
    slot = jnp.arange(TB_DEV, dtype=jnp.int32)
    first_src = jnp.take_along_axis(sperm, jnp.broadcast_to(slot % SB_DEV, (devices_all, TB_DEV)), axis=1)
    position = jax.vmap(lambda p: jnp.zeros((TB_DEV,), jnp.int32).at[p].set(slot))(tperm)
    pos_extra = jnp.take_along_axis(position, extra_t, axis=1)
    base_src = jnp.take_along_axis(sperm, pos_extra % SB_DEV, axis=1)
    shift = jax.random.randint(keys[3], (devices_all, TB_DEV), 0, SB_DEV - 1)
    extra_s = (base_src + 1 + shift) % SB_DEV
    sources = jnp.concatenate([first_src, extra_s], axis=1).astype(jnp.int32)
    targets = jnp.concatenate([tperm, extra_t], axis=1).astype(jnp.int32)
    draw_u = jax.random.randint(keys[4], (devices_all,), 0, TB_DEV + 1)
    counts = TB_DEV + draw_u * draw_u // TB_DEV
    pick = jax.random.randint(keys[5], (), 0, devices_all)
    other = (pick + 1 + jax.random.randint(keys[6], (), 0, devices_all - 1)) % devices_all
    index = jnp.arange(devices_all, dtype=jnp.int32)
    counts = jnp.where(index == pick, 2 * TB_DEV, counts)
    counts = jnp.where(index == other, TB_DEV, counts).astype(jnp.int32)
    return (sources.reshape(N_SRC, N_TGT, 2 * TB_DEV), targets.reshape(N_SRC, N_TGT, 2 * TB_DEV), counts.reshape(N_SRC, N_TGT))


def draw_pair_source(key, part):
    return pair_tables(key)[0]


def draw_pair_target(key, part):
    return pair_tables(key)[1]


def draw_pair_count(key, part):
    return pair_tables(key)[2]


def block_levels(rng, extent, cuts, low, largest):
    factor_of, own = 1.0, jax.random.fold_in(rng, 6)
    for axis_at, blocks in cuts:
        heights = jnp.exp(jax.random.uniform(jax.random.fold_in(own, axis_at), (blocks,), jnp.float32, low / len(cuts), largest / len(cuts)))
        factor_of = factor_of * jnp.repeat(heights, extent[axis_at] // blocks).reshape([-1 if axis == axis_at else 1 for axis in range(len(extent))])
    return factor_of


def noise(rng, dims, scale, bound, pieces=(), kind=jnp.bfloat16):
    level = block_levels(rng, dims, pieces, -0.22, 0.18) if pieces else 1.0
    values = jax.random.normal(rng, dims, jnp.float32) * scale * level
    return jnp.minimum(jnp.maximum(values, -bound), bound).astype(kind)


def setup_inputs(seed: int = 0) -> dict:
    splits = jax.random.split(jax.random.key(seed), 9)
    return {
        "source_points": noise(splits[0], (PC, NS), 0.3, 1.8, ((1, 512),), jnp.float32),
        "source_potential": draw_source_potential(jax.random.fold_in(splits[8], 71), 0),
        "source_logw": jnp.clip(jax.random.uniform(splits[2], (NS,), jnp.float32, -2.0, 2.0) * block_levels(splits[2], (NS,), ((0, 64),), -0.4, 0.0), -2.0, 2.0),
        "target_points": noise(splits[3], (PC, NT), 0.3, 1.8, ((1, 8),), jnp.float32),
        "target_logw": draw_target_logw(jax.random.fold_in(splits[8], 71), 0),
        "pair_source": draw_pair_source(jax.random.fold_in(splits[8], 71), 0),
        "pair_target": draw_pair_target(jax.random.fold_in(splits[8], 71), 0),
        "pair_count": draw_pair_count(jax.random.fold_in(splits[8], 71), 0),
    }


entropic = 0.5
lowest = -1.0e30
group_slots = 16


def reduce_pairs(own_pts, own_ids, far_pts, far_vals, far_ids, count, groups):
    width = own_pts.shape[0]
    own_blocks = own_pts.reshape(width, -1, BLOCK)
    far_blocks = far_pts.reshape(width, -1, BLOCK)
    far_rows = far_vals.reshape(-1, BLOCK)
    n_own = own_blocks.shape[1]
    own_sq = jnp.sum(own_blocks * own_blocks, axis=0)
    far_sq = jnp.sum(far_blocks * far_blocks, axis=0)
    owners = jnp.arange(n_own, dtype=jnp.int32)

    def step(k, carry):
        peak, total = carry
        start = (k * group_slots).astype(jnp.int32)
        own_g = lax.dynamic_slice_in_dim(own_ids, start, group_slots)
        far_g = lax.dynamic_slice_in_dim(far_ids, start, group_slots)
        valid = (start + jnp.arange(group_slots, dtype=jnp.int32)) < count
        own_sel = jnp.take(own_blocks, own_g, axis=1)
        far_sel = jnp.take(far_blocks, far_g, axis=1)
        cross = jnp.einsum("cga,cgb->gab", far_sel, own_sel, precision=lax.Precision.HIGHEST)
        cost = jnp.take(far_sq, far_g, axis=0)[:, :, None] + jnp.take(own_sq, own_g, axis=0)[:, None, :] - 2.0 * cross
        score = (jnp.take(far_rows, far_g, axis=0)[:, :, None] - cost) / entropic
        tile_peak = jnp.max(score, axis=1)
        tile_total = jnp.sum(jnp.exp(score - tile_peak[:, None, :]), axis=1)
        tile_peak = jnp.where(valid[:, None], tile_peak, lowest)
        tile_total = jnp.where(valid[:, None], tile_total, 0.0)
        match = (own_g[:, None] == owners[None, :]) & valid[:, None]
        spread = jnp.where(match[:, :, None], tile_peak[:, None, :], lowest)
        new_peak = jnp.maximum(peak, jnp.max(spread, axis=0))
        lifted = tile_total * jnp.exp(tile_peak - jnp.take(new_peak, own_g, axis=0))
        added = jnp.dot(match.T.astype(total.dtype), lifted, precision=lax.Precision.HIGHEST)
        return new_peak, total * jnp.exp(peak - new_peak) + added

    peak0 = jnp.full((n_own, BLOCK), lowest, own_pts.dtype)
    total0 = jnp.zeros((n_own, BLOCK), own_pts.dtype)
    return lax.fori_loop(0, groups, step, (peak0, total0))


def reference(source_points, source_potential, source_logw, target_points, target_logw, pair_source, pair_target, pair_count):
    groups = PAIRS // group_slots
    src_pts = source_points.reshape(PC, N_SRC, SB_DEV * BLOCK).transpose(1, 0, 2)
    tgt_pts = target_points.reshape(PC, N_TGT, TB_DEV * BLOCK).transpose(1, 0, 2)
    src_vals = source_potential.reshape(N_SRC, SB_DEV * BLOCK)

    def column_step(carry, items):
        peak, total = carry
        pts, vals, ids_src, ids_tgt, counts = items
        part_peak, part_total = jax.vmap(
            lambda tp, it, isrc, cnt: reduce_pairs(tp, it, pts, vals, isrc, cnt, groups)
        )(tgt_pts, ids_tgt, ids_src, counts)
        top = jnp.maximum(peak, part_peak)
        return (top, total * jnp.exp(peak - top) + part_total * jnp.exp(part_peak - top)), None

    init = (jnp.full((N_TGT, TB_DEV, BLOCK), lowest, jnp.float32), jnp.zeros((N_TGT, TB_DEV, BLOCK), jnp.float32))
    (peak, total), _ = lax.scan(column_step, init, (src_pts, src_vals, pair_source, pair_target, pair_count))
    col_lse = (peak + jnp.log(total)).reshape(-1)
    target_potential = entropic * target_logw - entropic * col_lse
    tgt_vals = target_potential.reshape(N_TGT, TB_DEV * BLOCK)

    def row_part(items):
        pts, ids_src, ids_tgt, counts = items
        part_peak, part_total = jax.vmap(
            lambda tp, tv, isrc, it, cnt: reduce_pairs(pts, isrc, tp, tv, it, cnt, groups)
        )(tgt_pts, tgt_vals, ids_src, ids_tgt, counts)
        top = jnp.max(part_peak, axis=0)
        summed = jnp.sum(part_total * jnp.exp(part_peak - top[None]), axis=0)
        return (top + jnp.log(summed)).reshape(-1)

    row_lse = lax.map(row_part, (src_pts, pair_source, pair_target, pair_count)).reshape(-1)
    updated_source = entropic * source_logw - entropic * row_lse
    return target_potential, updated_source
```

```python
import functools
import math

import jax
import jax.numpy as jnp
from jax import lax
from jax.experimental import pallas as pl
from jax.experimental.pallas import tpu as pltpu
from jax.sharding import PartitionSpec as P

BLOCK = 128
HALF = 64
ROW_U = 50
ROW_F = 54
LOG2E = 1.4426950408889634
LN2 = 0.6931471805599453
SCALE = 2.0 * LOG2E
ROOT = math.sqrt(2.0 * SCALE)
LOWEST = -1.0e30
UNROLL = 16
CHUNKS = 4
MESH = pl.DeviceIdType.MESH
f32 = jnp.float32
bf16 = jnp.bfloat16


def split(x):
    high = x.astype(bf16)
    return high, (x - high.astype(f32)).astype(bf16)


def residue(x):
    high, low = split(x)
    return x - high.astype(f32) - low.astype(f32)


def rows_of(value, shape):
    return jnp.broadcast_to(value, shape)


def merge(parts):
    top = jnp.max(parts, axis=0)
    return top + jnp.log2(jnp.sum(jnp.exp2(parts - top[None]), axis=0))


def pair_pass(slots, count, left_ids, right_ids, left, right, lse):
    def body(k, carry):
        for step in range(UNROLL):
            p = k * UNROLL + step
            a = left[left_ids[p]]
            r = right[right_ids[p]]
            lhs = jnp.concatenate([a, a], axis=1)
            rhs = jnp.concatenate([r[:HALF], r[:HALF], r[HALF:], r[HALF:]], axis=0)
            score = jnp.dot(lhs, rhs, preferred_element_type=f32)
            top = jnp.max(score, axis=0, keepdims=True)
            total = jnp.sum(jnp.exp2(score - top), axis=0, keepdims=True)
            lse[pl.ds(p, 1), :] = jnp.where(p < count, top + jnp.log2(total), LOWEST)
        return carry

    lax.fori_loop(0, slots // UNROLL, body, 0)


def owner_pass(owners, slots, ids, id_row, lse, peak, scaled):
    index = lax.broadcasted_iota(jnp.int32, (owners, BLOCK), 0)

    def lift(k, top):
        for step in range(8):
            p = k * 8 + step
            row = rows_of(lse[pl.ds(p, 1), :], (owners, BLOCK))
            top = jnp.maximum(top, jnp.where(index == ids[p], row, LOWEST))
        return top

    top = lax.fori_loop(0, slots // 8, lift, jnp.full((owners, BLOCK), LOWEST, f32))
    peak[0:owners, :] = top

    def scale(k, carry):
        tops = jnp.concatenate([peak[pl.ds(ids[k * 8 + step], 1), :] for step in range(8)], axis=0)
        rows = pl.ds(pl.multiple_of(k * 8, 8), 8)
        scaled[rows, :] = jnp.exp2(lse[rows, :] - tops)
        return carry

    lax.fori_loop(0, slots // 8, scale, 0)
    hit = lax.broadcasted_iota(jnp.int32, (owners, slots), 0) == id_row[...]
    pick = jnp.where(hit, 1.0, 0.0).astype(bf16)
    high, low = split(scaled[...])
    total = jnp.dot(pick, high, preferred_element_type=f32) + jnp.dot(
        pick, low, preferred_element_type=f32
    )
    return top + jnp.log2(total)


def kernel(
    dims,
    ids_src, ids_tgt, count_ref,
    row_src, row_tgt, spts, spot, slogw, tlogw, tpts_hbm,
    out_t, out_s,
    tpts, xbuf, r_tgt, a_tgt, r_src, a_src, y_sq, lse, peak, scaled,
    part, recv_y, comb, recv_z, full, rowpart, recv_x,
    load_sem, gather_send, gather_recv, y_send, y_recv, z_send, z_recv, g_send, g_recv, x_send, x_recv,
):
    ny, nz, nt, n_tb, n_sb, slots, pc = dims
    me_s, me_t = lax.axis_index("src"), lax.axis_index("tgt")
    my_y, my_z = lax.rem(me_s, ny), lax.div(me_s, ny)
    per_y = n_tb // ny
    shard_blocks = n_sb // nt
    count = count_ref[0]

    def along_y(d):
        return (my_z * ny + lax.rem(my_y + d, ny), me_t)

    def along_z(d):
        return (lax.rem(my_z + d, nz) * ny + my_y, me_t)

    def along_t(d):
        return (me_s, lax.rem(me_t + d, nt))

    barrier = pltpu.get_barrier_semaphore()
    peers = (
        [along_t(d) for d in range(1, nt)]
        + [along_y(d) for d in range(1, ny)]
        + [along_z(d) for d in range(1, nz)]
    )
    for peer in peers:
        pl.semaphore_signal(barrier, inc=1, device_id=peer, device_id_type=MESH)

    width = n_tb * BLOCK // CHUNKS
    loads = []
    for c in range(CHUNKS):
        cols = pl.ds(c * width, width)
        load = pltpu.make_async_copy(tpts_hbm.at[:, cols], tpts.at[:, cols], load_sem.at[c])
        load.start()
        loads.append(load)

    x = spts[...] * ROOT
    pot = spot[...]
    cells = pot.shape[1]
    u = SCALE * pot - 0.5 * jnp.sum(x * x, axis=0, keepdims=True)
    one = jnp.ones((1, cells), f32)
    xbuf[me_t] = jnp.concatenate([x, u, residue(u), one, one, pot, 0.0 * one], axis=0)

    pl.semaphore_wait(barrier, len(peers))

    def exchange(n, me, where, src, dst, send, recv):
        sent = []
        for d in range(1, n):
            copy = pltpu.make_async_remote_copy(
                src_ref=src(lax.rem(me + d, n)),
                dst_ref=dst(me),
                send_sem=send.at[d - 1],
                recv_sem=recv.at[me],
                device_id=where(d),
                device_id_type=MESH,
            )
            copy.start()
            sent.append(copy)
        return sent

    def collect(n, me, where, dst, send, recv):
        for d in range(1, n):
            other = lax.rem(me + d, n)
            pltpu.make_async_remote_copy(
                src_ref=dst(other),
                dst_ref=dst(other),
                send_sem=send.at[d - 1],
                recv_sem=recv.at[other],
                device_id=where(d),
                device_id_type=MESH,
            ).wait_recv()

    xslot = lambda t: xbuf.at[t]
    sent_g = exchange(nt, me_t, along_t, lambda t: xbuf.at[me_t], xslot, gather_send, gather_recv)

    tail = lax.broadcasted_iota(jnp.int32, (HALF - pc, BLOCK), 0)
    tail = jnp.where(tail < 2, 1.0, 0.0)

    def prepare(k, carry):
        for step in range(4):
            b = k * 4 + step
            y = tpts[:, pl.ds(pl.multiple_of(b * BLOCK, BLOCK), BLOCK)] * ROOT
            y_sq[pl.ds(b, 1), :] = 0.5 * jnp.sum(y * y, axis=0, keepdims=True)
            high, low = split(jnp.concatenate([y, tail], axis=0))
            r_tgt[b] = jnp.concatenate([high, low], axis=0)
        return carry

    per_chunk = n_tb // CHUNKS // 4
    for c in range(CHUNKS):
        loads[c].wait()
        lax.fori_loop(c * per_chunk, (c + 1) * per_chunk, prepare, 0)

    collect(nt, me_t, along_t, xslot, gather_send, gather_recv)
    zeros = jnp.zeros((HALF - 56, BLOCK), f32)
    for t in range(nt):
        for h in range(shard_blocks):
            b = t * shard_blocks + h
            xs = xbuf[t, :, h * BLOCK : (h + 1) * BLOCK]
            high, low = split(jnp.concatenate([xs, zeros], axis=0))
            both = jnp.concatenate([high, low], axis=0)
            r_src[b] = both
            a_src[b] = both.T

    pair_pass(slots, count, ids_src, ids_tgt, a_src, r_tgt, lse)
    part[...] = owner_pass(n_tb, slots, ids_tgt, row_tgt, lse, peak, scaled)

    band = lambda y: pl.ds(pl.multiple_of(y * per_y, per_y), per_y)
    yslot = lambda y: recv_y.at[y]
    sent_y = exchange(ny, my_y, along_y, lambda y: part.at[band(y)], yslot, y_send, y_recv)
    recv_y[my_y] = part[band(my_y), :]
    collect(ny, my_y, along_y, yslot, y_send, y_recv)
    comb[...] = merge(recv_y[...])
    zslot = lambda z: recv_z.at[z]
    sent_z = exchange(nz, my_z, along_z, lambda z: comb, zslot, z_send, z_recv)
    recv_z[my_z] = comb[...]
    collect(nz, my_z, along_z, zslot, z_send, z_recv)
    full[band(my_y), :] = merge(recv_z[...])
    gslot = lambda y: full.at[band(y)]
    sent_a = exchange(ny, my_y, along_y, lambda y: full.at[band(my_y)], gslot, g_send, g_recv)
    collect(ny, my_y, along_y, gslot, g_send, g_recv)

    total = full[...]
    out_t[...] = 0.5 * tlogw[...] - (0.5 * LN2) * (total - y_sq[...])
    peak[...] = LOG2E * tlogw[...] - total

    line = lax.broadcasted_iota(jnp.int32, (16, BLOCK), 0)

    def turn(k, carry):
        for step in range(4):
            b = k * 4 + step
            v = peak[pl.ds(b, 1), :]
            v_high, v_low = split(v)
            rest = residue(v)
            r = r_tgt[b]
            high = r[48:64].astype(f32)
            high = jnp.where(line == 4, v_high.astype(f32), jnp.where(line == 5, rest, high))
            low = jnp.where(line == 4, v_low.astype(f32), r[112:128].astype(f32))
            both = jnp.concatenate([r[:48], high.astype(bf16), r[64:112], low.astype(bf16)], axis=0)
            a_tgt[b] = both.T
        return carry

    lax.fori_loop(0, n_tb // 4, turn, 0)

    pair_pass(slots, count, ids_tgt, ids_src, a_tgt, r_src, lse)
    rowpart[...] = owner_pass(n_sb, slots, ids_src, row_src, lse, peak, scaled)
    rslot = lambda t: recv_x.at[t]
    sent_x = exchange(nt, me_t, along_t, lambda t: rowpart, rslot, x_send, x_recv)
    recv_x[me_t] = rowpart[...]
    collect(nt, me_t, along_t, rslot, x_send, x_recv)
    result = merge(recv_x[...])
    potential = jnp.concatenate(
        [
            xbuf[t, ROW_F : ROW_F + 1, h * BLOCK : (h + 1) * BLOCK]
            for t in range(nt)
            for h in range(shard_blocks)
        ],
        axis=0,
    )
    out_s[...] = potential + 0.5 * slogw[...] - (0.5 * LN2) * result
    for copy in sent_g + sent_y + sent_z + sent_a + sent_x:
        copy.wait_send()


def local(
    n_src,
    n_tgt,
    source_points,
    source_potential,
    source_logw,
    target_points,
    target_logw,
    pair_source,
    pair_target,
    pair_count,
):
    pc, cells = source_points.shape
    n_tb = target_points.shape[1] // BLOCK
    n_sb = source_logw.shape[0] // BLOCK
    slots = pair_source.shape[-1]
    ny = math.isqrt(n_src)
    nz = n_src // ny
    nt = n_tgt
    per_y = n_tb // ny
    vmem = pl.BlockSpec(memory_space=pltpu.VMEM)
    smem = pl.BlockSpec(memory_space=pltpu.SMEM)
    dma = pltpu.SemaphoreType.DMA
    ids_src, ids_tgt = pair_source.reshape(-1), pair_target.reshape(-1)
    out_t, out_s = pl.pallas_call(
        functools.partial(kernel, (ny, nz, nt, n_tb, n_sb, slots, pc)),
        out_shape=(
            jax.ShapeDtypeStruct((n_tb, BLOCK), f32),
            jax.ShapeDtypeStruct((n_sb, BLOCK), f32),
        ),
        in_specs=[smem] * 3 + [vmem] * 6 + [pl.BlockSpec(memory_space=pl.ANY)],
        out_specs=(vmem, vmem),
        scratch_shapes=[
            pltpu.VMEM((pc, n_tb * BLOCK), f32),
            pltpu.VMEM((nt, 56, cells), f32),
            pltpu.VMEM((n_tb, BLOCK, BLOCK), bf16),
            pltpu.VMEM((n_tb, BLOCK, BLOCK), bf16),
            pltpu.VMEM((n_sb, BLOCK, BLOCK), bf16),
            pltpu.VMEM((n_sb, BLOCK, BLOCK), bf16),
            pltpu.VMEM((n_tb, BLOCK), f32),
            pltpu.VMEM((slots, BLOCK), f32),
            pltpu.VMEM((n_tb, BLOCK), f32),
            pltpu.VMEM((slots, BLOCK), f32),
            pltpu.VMEM((n_tb, BLOCK), f32),
            pltpu.VMEM((ny, per_y, BLOCK), f32),
            pltpu.VMEM((per_y, BLOCK), f32),
            pltpu.VMEM((nz, per_y, BLOCK), f32),
            pltpu.VMEM((n_tb, BLOCK), f32),
            pltpu.VMEM((n_sb, BLOCK), f32),
            pltpu.VMEM((nt, n_sb, BLOCK), f32),
            dma((CHUNKS,)),
            dma((nt,)), dma((nt,)),
            dma((ny,)), dma((ny,)),
            dma((nz,)), dma((nz,)),
            dma((ny,)), dma((ny,)),
            dma((nt,)), dma((nt,)),
        ],
        compiler_params=pltpu.CompilerParams(
            collective_id=0, has_side_effects=True, vmem_limit_bytes=40 * 2**20
        ),
    )(
        ids_src,
        ids_tgt,
        pair_count.reshape(-1),
        ids_src.reshape(1, slots),
        ids_tgt.reshape(1, slots),
        source_points,
        source_potential.reshape(1, cells),
        source_logw.reshape(n_sb, BLOCK),
        target_logw.reshape(n_tb, BLOCK),
        target_points,
    )
    return out_t.reshape(-1), out_s.reshape(-1)


def solution(mesh):
    placed = (
        P(None, ("src", "tgt")),
        P(("src", "tgt")),
        P("src"),
        P(None, "tgt"),
        P("tgt"),
        P("src", "tgt", None),
        P("src", "tgt", None),
        P("src", "tgt"),
    )
    return jax.shard_map(
        functools.partial(local, mesh.shape["src"], mesh.shape["tgt"]),
        mesh=mesh,
        in_specs=placed,
        out_specs=(P("tgt"), P("src")),
        check_vma=False,
    )
```

```python
import functools
import math

import jax
import jax.numpy as jnp
from jax import lax
from jax.experimental import pallas as pl
from jax.experimental.pallas import tpu as pltpu
from jax.sharding import PartitionSpec as P

BLOCK = 128
HALF = 64
ROW_U = 50
ROW_F = 54
LOG2E = 1.4426950408889634
LN2 = 0.6931471805599453
SCALE = 2.0 * LOG2E
ROOT = math.sqrt(2.0 * SCALE)
LOWEST = -1.0e30
UNROLL = 32
CHUNKS = 4
MESH = pl.DeviceIdType.MESH
f32 = jnp.float32
bf16 = jnp.bfloat16


def split(x):
    high = x.astype(bf16)
    return high, (x - high.astype(f32)).astype(bf16)


def residue(x):
    high, low = split(x)
    return x - high.astype(f32) - low.astype(f32)


def merge(parts):
    top = jnp.max(parts, axis=0)
    return top + jnp.log2(jnp.sum(jnp.exp2(parts - top[None]), axis=0))


def column_lse(a, r):
    lhs = jnp.concatenate([a, a], axis=1)
    rhs = jnp.concatenate([r[:HALF], r[:HALF], r[HALF:], r[HALF:]], axis=0)
    score = jnp.dot(lhs, rhs, preferred_element_type=f32)
    top = jnp.max(score, axis=0, keepdims=True)
    return top + jnp.log2(jnp.sum(jnp.exp2(score - top), axis=0, keepdims=True))


def owner_pass(owners, first, slots, id_of, id_row, lse, peak, scaled):
    index = lax.broadcasted_iota(jnp.int32, (owners, BLOCK), 0)

    def lift(k, top):
        for step in range(8):
            p = first + k * 8 + step
            row = jnp.broadcast_to(lse[pl.ds(p, 1), :], (owners, BLOCK))
            top = jnp.maximum(top, jnp.where(index == id_of(p), row, LOWEST))
        return top

    top = lax.fori_loop(0, slots // 8, lift, jnp.full((owners, BLOCK), LOWEST, f32))
    peak[0:owners, :] = top

    def scale(k, carry):
        at = first + k * 16
        tops = jnp.concatenate([peak[pl.ds(id_of(at + step), 1), :] for step in range(16)], axis=0)
        rows = pl.ds(pl.multiple_of(at, 16), 16)
        scaled[rows, :] = jnp.exp2(lse[rows, :] - tops)
        return carry

    lax.fori_loop(0, slots // 16, scale, 0)
    hit = lax.broadcasted_iota(jnp.int32, (owners, slots), 0) == id_row
    pick = jnp.where(hit, 1.0, 0.0).astype(bf16)
    high, low = split(scaled[first : first + slots, :])
    total = jnp.dot(pick, high, preferred_element_type=f32) + jnp.dot(
        pick, low, preferred_element_type=f32
    )
    return top + jnp.log2(total)


def kernel(
    dims,
    spts_hbm, spot_hbm, slogw_hbm, tpts_hbm, tlogw_hbm, src_hbm, tgt_hbm, count_hbm,
    out_t, out_s,
    spts, spot, slogw, tlogw, ids_src, ids_tgt, count_ref, row_src, row_tgt, base_vec, base_src,
    tpts, xbuf, r_tgt, a_tgt, r_src, a_src, y_sq, lse, peak, scaled,
    extra, part, recv_y, comb, recv_z, full, rowpart, recv_x,
    load_sem, chunk_sem, base_sem, gather_send, gather_recv, relay_send,
    y_send, y_recv, z_send, z_recv, g_send, g_recv, x_send, x_recv,
):
    ny, nz, nt, n_tb, n_sb, slots, pc = dims
    nx = nt // 2
    me_s, me_t = lax.axis_index("src"), lax.axis_index("tgt")
    my_y, my_z = lax.rem(me_s, ny), lax.div(me_s, ny)
    my_x, my_c = lax.div(me_t, 2), lax.rem(me_t, 2)
    per_y = n_tb // ny
    shard_blocks = n_sb // nt
    n_extra = slots - n_tb

    def along_y(d):
        return (my_z * ny + lax.rem(my_y + d, ny), me_t)

    def along_z(d):
        return (lax.rem(my_z + d, nz) * ny + my_y, me_t)

    def along_t(d):
        return (me_s, lax.rem(me_t + d, nt))

    barrier = pltpu.get_barrier_semaphore()
    peers = (
        [along_t(d) for d in range(1, nt)]
        + [along_y(d) for d in range(1, ny)]
        + [along_z(d) for d in range(1, nz)]
    )
    for peer in peers:
        pl.semaphore_signal(barrier, inc=1, device_id=peer, device_id_type=MESH)

    pairs = [
        (spts_hbm, spts), (spot_hbm, spot), (src_hbm.at[0], row_src), (tgt_hbm.at[0], row_tgt),
        (src_hbm.at[0], ids_src), (tgt_hbm.at[0], ids_tgt), (count_hbm, count_ref),
        (slogw_hbm, slogw), (tlogw_hbm, tlogw),
    ]
    small = [pltpu.make_async_copy(a, b, load_sem.at[k]) for k, (a, b) in enumerate(pairs)]
    for load in small:
        load.start()
    width = n_tb * BLOCK // CHUNKS
    loads = []
    for c in range(CHUNKS):
        cols = pl.ds(c * width, width)
        load = pltpu.make_async_copy(tpts_hbm.at[:, cols], tpts.at[:, cols], chunk_sem.at[c])
        load.start()
        loads.append(load)
    small[0].wait()
    small[1].wait()

    x = spts[...] * ROOT
    pot = spot[...]
    cells = pot.shape[1]
    u = SCALE * pot - 0.5 * jnp.sum(x * x, axis=0, keepdims=True)
    one = jnp.ones((1, cells), f32)
    xbuf[me_t] = jnp.concatenate([x, u, residue(u), one, one, pot, 0.0 * one], axis=0)

    pl.semaphore_wait(barrier, len(peers))

    def remote(src, dst, send, recv, where):
        return pltpu.make_async_remote_copy(
            src_ref=src, dst_ref=dst, send_sem=send, recv_sem=recv,
            device_id=where, device_id_type=MESH,
        )

    def chip(d):
        return (me_s, lax.rem(my_x + d, nx) * 2 + my_c)

    other_core = (me_s, my_x * 2 + 1 - my_c)
    mine = xbuf.at[me_t]
    order = sorted(range(1, nx), key=lambda d: -min(d, nx - d))
    sent = [remote(mine, mine, gather_send.at[d], gather_recv.at[me_t], chip(d)) for d in order]
    sent.append(remote(mine, mine, gather_send.at[0], gather_recv.at[me_t], other_core))
    for copy in sent:
        copy.start()

    def arrived(slot, sem, where):
        remote(slot, slot, gather_send.at[0], sem, where).wait_recv()

    for load in small[2:]:
        load.wait()
    count = count_ref[0, 0]
    turned_t = jnp.broadcast_to(row_tgt[:, 0:n_tb], (n_tb, n_tb)).T
    turned_s = jnp.broadcast_to(row_src[:, 0:n_tb], (n_tb, n_tb)).T
    owner = lax.broadcasted_iota(jnp.int32, (n_tb, n_tb), 1)
    base_vec[...] = jnp.sum(jnp.where(turned_t == owner, turned_s, 0), axis=0, keepdims=True)
    base_copy = pltpu.make_async_copy(base_vec, base_src, base_sem)
    base_copy.start()

    tail = lax.broadcasted_iota(jnp.int32, (HALF - pc, BLOCK), 0)
    tail = jnp.where(tail < 2, 1.0, 0.0)

    def prepare(k, carry):
        for step in range(4):
            b = k * 4 + step
            y = tpts[:, pl.ds(pl.multiple_of(b * BLOCK, BLOCK), BLOCK)] * ROOT
            y_sq[pl.ds(b, 1), :] = 0.5 * jnp.sum(y * y, axis=0, keepdims=True)
            high, low = split(jnp.concatenate([y, tail], axis=0))
            r_tgt[b] = jnp.concatenate([high, low], axis=0)
        return carry

    per_chunk = n_tb // CHUNKS // 4
    for c in range(CHUNKS):
        loads[c].wait()
        lax.fori_loop(c * per_chunk, (c + 1) * per_chunk, prepare, 0)

    zeros = jnp.zeros((HALF - 56, BLOCK), f32)

    def source(t):
        for h in range(shard_blocks):
            b = t * shard_blocks + h
            xs = xbuf[t, :, h * BLOCK : (h + 1) * BLOCK]
            high, low = split(jnp.concatenate([xs, zeros], axis=0))
            both = jnp.concatenate([high, low], axis=0)
            r_src[b] = both
            a_src[b] = both.T

    source(me_t)
    relays = []
    for d in reversed(order):
        t = lax.rem(my_x + d, nx) * 2 + my_c
        arrived(xbuf.at[t], gather_recv.at[t], chip(d))
        relay = remote(xbuf.at[t], xbuf.at[t], relay_send.at[d], gather_recv.at[t], other_core)
        relay.start()
        relays.append(relay)
        source(t)
    for d in [0] + order[::-1]:
        t = lax.rem(my_x + d, nx) * 2 + 1 - my_c
        arrived(xbuf.at[t], gather_recv.at[t], other_core)
        source(t)
    base_copy.wait()

    def far_columns(k, carry):
        for step in range(UNROLL):
            p = n_tb + k * UNROLL + step
            row = column_lse(a_src[ids_src[0, p]], r_tgt[ids_tgt[0, p]])
            lse[pl.ds(p, 1), :] = jnp.where(p < count, row, LOWEST)
        return carry

    lax.fori_loop(0, n_extra // UNROLL, far_columns, 0)
    extra[...] = owner_pass(
        n_tb, n_tb, n_extra, lambda p: ids_tgt[0, p], row_tgt[:, n_tb:], lse, peak, scaled
    )

    def band(y):
        return pl.ds(pl.multiple_of(y * per_y, per_y), per_y)

    def to_y(d):
        y = lax.rem(my_y + d, ny)
        return remote(part.at[band(y)], recv_y.at[my_y], y_send.at[d], y_recv.at[my_y], along_y(d))

    def near_columns(m, carry):
        ds = (ny // 2 - m, lax.rem(ny // 2 + 1 + m, ny))
        for d in ds:
            start = lax.rem(my_y + d, ny) * per_y
            for step in range(per_y):
                b = start + step
                lse[pl.ds(b, 1), :] = column_lse(a_src[base_src[0, b]], r_tgt[b])
        for d in ds:
            rows = band(lax.rem(my_y + d, ny))
            part[rows, :] = merge(jnp.stack([lse[rows, :], extra[rows, :]]))
        to_y(ds[0]).start()

        @pl.when(m < ny // 2 - 1)
        def _():
            to_y(ds[1]).start()

        return carry

    lax.fori_loop(0, ny // 2, near_columns, 0)
    recv_y[my_y] = part[band(my_y), :]

    def collect(n, me, where, dst, send, recv):
        for d in range(1, n):
            other = lax.rem(me + d, n)
            remote(dst(other), dst(other), send.at[d], recv.at[other], where(d)).wait_recv()

    collect(ny, my_y, along_y, lambda y: recv_y.at[y], y_send, y_recv)
    comb[...] = merge(recv_y[...])

    def to_z(d):
        return remote(comb, recv_z.at[my_z], z_send.at[d], z_recv.at[my_z], along_z(d))

    def by_distance(n):
        return sorted(range(1, n), key=lambda d: -min(d, n - d))

    for d in by_distance(nz):
        to_z(d).start()
    recv_z[my_z] = comb[...]
    collect(nz, my_z, along_z, lambda z: recv_z.at[z], z_send, z_recv)
    full[band(my_y), :] = merge(recv_z[...])

    def to_all(d):
        rows = full.at[band(my_y)]
        return remote(rows, rows, g_send.at[d], g_recv.at[my_y], along_y(d))

    for d in by_distance(ny):
        to_all(d).start()

    line = lax.broadcasted_iota(jnp.int32, (16, BLOCK), 0)

    def near_rows(k, carry):
        d = lax.rem(lax.div(k + 1, 2) * (1 - 2 * lax.rem(k + 1, 2)) * -1 + 2 * ny, ny)
        y = lax.rem(my_y + d, ny)
        rows = band(y)

        @pl.when(k > 0)
        def _():
            slot = full.at[rows]
            remote(slot, slot, g_send.at[d], g_recv.at[y], along_y(d)).wait_recv()

        total = full[rows, :]
        weight = tlogw[rows, :]
        out_t[rows, :] = 0.5 * weight - (0.5 * LN2) * (total - y_sq[rows, :])
        v = LOG2E * weight - total
        v_high, v_low = split(v)
        rest = residue(v)
        v_high, v_low = v_high.astype(f32), v_low.astype(f32)
        for step in range(per_y):
            b = y * per_y + step
            r = r_tgt[b]
            one = slice(step, step + 1)
            high = jnp.where(line == 5, rest[one], r[48:64].astype(f32))
            high = jnp.where(line == 4, v_high[one], high)
            low = jnp.where(line == 4, v_low[one], r[112:128].astype(f32))
            both = jnp.concatenate([r[:48], high.astype(bf16), r[64:112], low.astype(bf16)], axis=0)
            turned = both.T
            a_tgt[b] = turned
            lse[pl.ds(b, 1), :] = column_lse(turned, r_src[base_src[0, b]])
        return carry

    lax.fori_loop(0, ny, near_rows, 0)

    def far_rows(k, carry):
        for step in range(UNROLL):
            p = n_tb + k * UNROLL + step
            row = column_lse(a_tgt[ids_tgt[0, p]], r_src[ids_src[0, p]])
            lse[pl.ds(p, 1), :] = jnp.where(p < count, row, LOWEST)
        return carry

    lax.fori_loop(0, n_extra // UNROLL, far_rows, 0)
    near = owner_pass(n_sb, 0, n_tb, lambda p: base_src[0, p], base_vec[...], lse, peak, scaled)
    far = owner_pass(
        n_sb, n_tb, n_extra, lambda p: ids_src[0, p], row_src[:, n_tb:], lse, peak, scaled
    )
    rowpart[...] = merge(jnp.stack([near, far]))

    def to_t(d):
        return remote(rowpart, recv_x.at[me_t], x_send.at[d], x_recv.at[me_t], along_t(d))

    for d in by_distance(nt):
        to_t(d).start()
    recv_x[me_t] = rowpart[...]
    potential = jnp.concatenate(
        [
            xbuf[t, ROW_F : ROW_F + 1, h * BLOCK : (h + 1) * BLOCK]
            for t in range(nt)
            for h in range(shard_blocks)
        ],
        axis=0,
    )
    collect(nt, me_t, along_t, lambda t: recv_x.at[t], x_send, x_recv)
    out_s[...] = potential + 0.5 * slogw[...] - (0.5 * LN2) * merge(recv_x[...])

    for copy in sent + relays:
        copy.wait_send()
    for n, to in ((ny, to_y), (nz, to_z), (ny, to_all), (nt, to_t)):
        for d in range(1, n):
            to(d).wait_send()


def local(
    n_src,
    n_tgt,
    source_points,
    source_potential,
    source_logw,
    target_points,
    target_logw,
    pair_source,
    pair_target,
    pair_count,
):
    pc, cells = source_points.shape
    n_tb = target_points.shape[1] // BLOCK
    n_sb = source_logw.shape[0] // BLOCK
    slots = pair_source.shape[-1]
    ny = math.isqrt(n_src)
    nz = n_src // ny
    nt = n_tgt
    per_y = n_tb // ny
    vmem = pl.BlockSpec(memory_space=pltpu.VMEM)
    dma = pltpu.SemaphoreType.DMA
    out_t, out_s = pl.pallas_call(
        functools.partial(kernel, (ny, nz, nt, n_tb, n_sb, slots, pc)),
        out_shape=(
            jax.ShapeDtypeStruct((n_tb, BLOCK), f32),
            jax.ShapeDtypeStruct((n_sb, BLOCK), f32),
        ),
        in_specs=[pl.BlockSpec(memory_space=pltpu.HBM)] * 8,
        out_specs=(vmem, vmem),
        scratch_shapes=[
            pltpu.VMEM((pc, cells), f32),
            pltpu.VMEM((1, cells), f32),
            pltpu.VMEM((n_sb, BLOCK), f32),
            pltpu.VMEM((n_tb, BLOCK), f32),
            pltpu.SMEM((1, slots), jnp.int32),
            pltpu.SMEM((1, slots), jnp.int32),
            pltpu.SMEM((1, 1), jnp.int32),
            pltpu.VMEM((1, slots), jnp.int32),
            pltpu.VMEM((1, slots), jnp.int32),
            pltpu.VMEM((1, n_tb), jnp.int32),
            pltpu.SMEM((1, n_tb), jnp.int32),
            pltpu.VMEM((pc, n_tb * BLOCK), f32),
            pltpu.VMEM((nt, 56, cells), f32),
            pltpu.VMEM((n_tb, BLOCK, BLOCK), bf16),
            pltpu.VMEM((n_tb, BLOCK, BLOCK), bf16),
            pltpu.VMEM((n_sb, BLOCK, BLOCK), bf16),
            pltpu.VMEM((n_sb, BLOCK, BLOCK), bf16),
            pltpu.VMEM((n_tb, BLOCK), f32),
            pltpu.VMEM((slots, BLOCK), f32),
            pltpu.VMEM((n_tb, BLOCK), f32),
            pltpu.VMEM((slots, BLOCK), f32),
            pltpu.VMEM((n_tb, BLOCK), f32),
            pltpu.VMEM((n_tb, BLOCK), f32),
            pltpu.VMEM((ny, per_y, BLOCK), f32),
            pltpu.VMEM((per_y, BLOCK), f32),
            pltpu.VMEM((nz, per_y, BLOCK), f32),
            pltpu.VMEM((n_tb, BLOCK), f32),
            pltpu.VMEM((n_sb, BLOCK), f32),
            pltpu.VMEM((nt, n_sb, BLOCK), f32),
            dma((9,)),
            dma((CHUNKS,)),
            dma,
            dma((nt,)), dma((nt,)), dma((nt,)),
            dma((ny,)), dma((ny,)),
            dma((nz,)), dma((nz,)),
            dma((ny,)), dma((ny,)),
            dma((nt,)), dma((nt,)),
        ],
        compiler_params=pltpu.CompilerParams(
            collective_id=0, has_side_effects=True, vmem_limit_bytes=60 * 2**20
        ),
    )(
        source_points,
        source_potential.reshape(1, cells),
        source_logw.reshape(n_sb, BLOCK),
        target_points,
        target_logw.reshape(n_tb, BLOCK),
        pair_source,
        pair_target,
        pair_count,
    )
    return out_t.reshape(-1), out_s.reshape(-1)


def solution(mesh):
    placed = (
        P(None, ("src", "tgt")),
        P(("src", "tgt")),
        P("src"),
        P(None, "tgt"),
        P("tgt"),
        P("src", "tgt", None),
        P("src", "tgt", None),
        P("src", "tgt"),
    )
    return jax.shard_map(
        functools.partial(local, mesh.shape["src"], mesh.shape["tgt"]),
        mesh=mesh,
        in_specs=placed,
        out_specs=(P("tgt"), P("src")),
        check_vma=False,
    )
```

```python
import functools
import math

import jax
import jax.numpy as jnp
from jax import lax
from jax.experimental import pallas as pl
from jax.experimental.pallas import tpu as pltpu
from jax.sharding import PartitionSpec as P

BLOCK = 128
HALF = 64
ROW_U = 50
ROW_F = 54
LOG2E = 1.4426950408889634
LN2 = 0.6931471805599453
SCALE = 2.0 * LOG2E
ROOT = math.sqrt(2.0 * SCALE)
LOWEST = -1.0e30
STEP = 64.0
MIDDLE = 6.0
UNROLL = 128
CHUNKS = 4
MESH = pl.DeviceIdType.MESH
f32 = jnp.float32
bf16 = jnp.bfloat16


def split(x):
    high = x.astype(bf16)
    return high, (x - high.astype(f32)).astype(bf16)


def residue(x):
    high, low = split(x)
    return x - high.astype(f32) - low.astype(f32)


def merge(parts):
    top = jnp.max(parts, axis=0)
    return top + jnp.log2(jnp.sum(jnp.exp2(parts - top[None]), axis=0))


def column_lse(a, r):
    lhs = jnp.concatenate([a, a], axis=1)
    rhs = jnp.concatenate([r[:HALF], r[:HALF], r[HALF:], r[HALF:]], axis=0)
    score = jnp.dot(lhs, rhs, preferred_element_type=f32)
    top = jnp.max(score, axis=0, keepdims=True)
    return top + jnp.log2(jnp.sum(jnp.exp2(score - top), axis=0, keepdims=True))


def raise_peaks(top, rows, ids):
    index = lax.broadcasted_iota(jnp.int32, top.shape, 0)
    tops = [top]
    for row, owner in zip(rows, ids):
        tops.append(jnp.where(index == owner, jnp.broadcast_to(row, top.shape), LOWEST))
    while len(tops) > 1:
        tops = [functools.reduce(jnp.maximum, tops[i : i + 2]) for i in range(0, len(tops), 2)]
    return tops[0]


def owner_sums(top, lse, pick, gather):
    high, low = split(top)
    parts = [high, low, residue(top).astype(bf16)]
    spare = gather.shape[1] - 3 * top.shape[0]
    if spare > 0:
        parts.append(jnp.zeros((spare, BLOCK), bf16))
    tops = jnp.dot(gather[...], jnp.concatenate(parts, axis=0), preferred_element_type=f32)
    high, low = split(jnp.exp2(lse - tops))
    total = jnp.dot(pick[...], high, preferred_element_type=f32) + jnp.dot(
        pick[...], low, preferred_element_type=f32
    )
    return top + jnp.log2(total)


def owner_steps(lse, pick, gather):
    step = jnp.clip(jnp.floor(lse * (1.0 / STEP)) - MIDDLE, -30.0, 30.0)
    power = jnp.where(lse > 0.5 * LOWEST, jnp.exp2(4.0 * step), 0.0)
    total = jnp.dot(pick[...], power.astype(bf16), preferred_element_type=f32)
    largest = jnp.floor(0.25 * (jnp.log2(jnp.maximum(total, 2.0**-122)) + 0.04))
    edge = STEP * (largest + MIDDLE + 1.0)
    edges = jnp.dot(gather[...], edge.astype(bf16), preferred_element_type=f32)
    high, low = split(jnp.exp2(lse - edges))
    total = jnp.dot(pick[...], high, preferred_element_type=f32) + jnp.dot(
        pick[...], low, preferred_element_type=f32
    )
    return edge + jnp.log2(total)


def kernel(
    dims,
    spts_hbm, spot_hbm, slogw_hbm, tpts_hbm, tlogw_hbm, src_hbm, tgt_hbm, count_hbm,
    out_t, out_s,
    spts, spot, slogw, tlogw, ids_src, ids_tgt, count_ref, row_src, row_tgt, base_vec, row_ids,
    tpts, xbuf, r_tgt, a_tgt, r_src, a_src, y_sq, lse, far, pick_t, gather_t, pick_s, gather_s,
    extra, part, recv_y, comb, recv_z, full, rowpart, recv_x,
    load_sem, chunk_sem, base_sem, gather_send, gather_recv, relay_send,
    y_send, y_recv, z_send, z_recv, g_send, g_recv, x_send, x_recv,
):
    ny, nz, nt, n_tb, n_sb, slots, pc = dims
    nx = nt // 2
    me_s, me_t = lax.axis_index("src"), lax.axis_index("tgt")
    my_y, my_z = lax.rem(me_s, ny), lax.div(me_s, ny)
    my_x, my_c = lax.div(me_t, 2), lax.rem(me_t, 2)
    per_y = n_tb // ny
    shard_blocks = n_sb // nt
    n_extra = slots - n_tb

    def along_y(d):
        return (my_z * ny + lax.rem(my_y + d, ny), me_t)

    def along_z(d):
        return (lax.rem(my_z + d, nz) * ny + my_y, me_t)

    def along_t(d):
        return (me_s, lax.rem(me_t + d, nt))

    barrier = pltpu.get_barrier_semaphore()
    peers = (
        [along_t(d) for d in range(1, nt)]
        + [along_y(d) for d in range(1, ny)]
        + [along_z(d) for d in range(1, nz)]
    )
    for peer in peers:
        pl.semaphore_signal(barrier, inc=1, device_id=peer, device_id_type=MESH)

    pairs = [
        (spts_hbm, spts), (spot_hbm, spot), (src_hbm.at[0], row_src), (tgt_hbm.at[0], row_tgt),
        (src_hbm.at[0], ids_src), (tgt_hbm.at[0], ids_tgt), (count_hbm, count_ref),
        (slogw_hbm, slogw), (tlogw_hbm, tlogw),
    ]
    small = [pltpu.make_async_copy(a, b, load_sem.at[k]) for k, (a, b) in enumerate(pairs)]
    for load in small:
        load.start()
    width = n_tb * BLOCK // CHUNKS
    loads = []
    for c in range(CHUNKS):
        cols = pl.ds(c * width, width)
        load = pltpu.make_async_copy(tpts_hbm.at[:, cols], tpts.at[:, cols], chunk_sem.at[c])
        load.start()
        loads.append(load)
    small[0].wait()
    small[1].wait()

    x = spts[...] * ROOT
    pot = spot[...]
    cells = pot.shape[1]
    u = SCALE * pot - 0.5 * jnp.sum(x * x, axis=0, keepdims=True)
    one = jnp.ones((1, cells), f32)
    xbuf[me_t] = jnp.concatenate([x, u, residue(u), one, one, pot, 0.0 * one], axis=0)

    pl.semaphore_wait(barrier, len(peers))

    def remote(src, dst, send, recv, where):
        return pltpu.make_async_remote_copy(
            src_ref=src, dst_ref=dst, send_sem=send, recv_sem=recv,
            device_id=where, device_id_type=MESH,
        )

    def chip(d):
        return (me_s, lax.rem(my_x + d, nx) * 2 + my_c)

    other_core = (me_s, my_x * 2 + 1 - my_c)
    mine = xbuf.at[me_t]
    order = sorted(range(1, nx), key=lambda d: -min(d, nx - d))
    sent = [remote(mine, mine, gather_send.at[d], gather_recv.at[me_t], chip(d)) for d in order]
    sent.append(remote(mine, mine, gather_send.at[0], gather_recv.at[me_t], other_core))
    for copy in sent:
        copy.start()

    def arrived(slot, sem, where):
        remote(slot, slot, gather_send.at[0], sem, where).wait_recv()

    for load in small[2:]:
        load.wait()
    count = count_ref[0, 0]
    turned_t = jnp.broadcast_to(row_tgt[:, 0:n_tb], (n_tb, n_tb)).T
    turned_s = jnp.broadcast_to(row_src[:, 0:n_tb], (n_tb, n_tb)).T
    owner = lax.broadcasted_iota(jnp.int32, (n_tb, n_tb), 1)
    base_row = jnp.sum(jnp.where(turned_t == owner, turned_s, 0), axis=0, keepdims=True)
    base_vec[:, 0:n_tb] = base_row
    base_vec[:, n_tb:] = row_src[:, n_tb:]
    base_copy = pltpu.make_async_copy(base_vec, row_ids, base_sem)
    base_copy.start()

    def one_hot(flags):
        return jnp.where(flags, 1.0, 0.0).astype(bf16)

    further_t, further_s = row_tgt[:, n_tb:], row_src[:, n_tb:]
    pick_t[...] = one_hot(lax.broadcasted_iota(jnp.int32, (n_tb, n_extra), 0) == further_t)
    column = jnp.broadcast_to(further_t, (n_tb, n_extra)).T
    gather_t[...] = one_hot(lax.broadcasted_iota(jnp.int32, (n_extra, n_tb), 1) == column)
    lane = lax.broadcasted_iota(jnp.int32, (BLOCK, BLOCK), 1)
    lane = jnp.where(lane < 3 * n_sb, lax.rem(lane, n_sb), -1)
    for at, ids in ((0, base_row), (n_tb, further_s)):
        n = ids.shape[1]
        pick_s[:, at : at + n] = one_hot(lax.broadcasted_iota(jnp.int32, (n_sb, n), 0) == ids)
        gather_s[at : at + n, :] = one_hot(jnp.broadcast_to(ids, (BLOCK, n)).T == lane[0:n])

    tail = lax.broadcasted_iota(jnp.int32, (HALF - pc, BLOCK), 0)
    tail = jnp.where(tail < 2, 1.0, 0.0)

    def prepare(k, carry):
        for step in range(4):
            b = k * 4 + step
            y = tpts[:, pl.ds(pl.multiple_of(b * BLOCK, BLOCK), BLOCK)] * ROOT
            y_sq[pl.ds(b, 1), :] = 0.5 * jnp.sum(y * y, axis=0, keepdims=True)
            high, low = split(jnp.concatenate([y, tail], axis=0))
            r_tgt[b] = jnp.concatenate([high, low], axis=0)
        return carry

    per_chunk = n_tb // CHUNKS // 4
    for c in range(CHUNKS):
        loads[c].wait()
        lax.fori_loop(c * per_chunk, (c + 1) * per_chunk, prepare, 0)

    zeros = jnp.zeros((HALF - 56, BLOCK), f32)

    def source(t):
        for h in range(shard_blocks):
            b = t * shard_blocks + h
            xs = xbuf[t, :, h * BLOCK : (h + 1) * BLOCK]
            high, low = split(jnp.concatenate([xs, zeros], axis=0))
            both = jnp.concatenate([high, low], axis=0)
            r_src[b] = both
            a_src[b] = both.T

    source(me_t)
    relays = []
    for d in reversed(order):
        t = lax.rem(my_x + d, nx) * 2 + my_c
        arrived(xbuf.at[t], gather_recv.at[t], chip(d))
        relay = remote(xbuf.at[t], xbuf.at[t], relay_send.at[d], gather_recv.at[t], other_core)
        relay.start()
        relays.append(relay)
        source(t)
    for d in [0] + order[::-1]:
        t = lax.rem(my_x + d, nx) * 2 + 1 - my_c
        arrived(xbuf.at[t], gather_recv.at[t], other_core)
        source(t)
    base_copy.wait()

    def far_columns(k, carry):
        for step in range(UNROLL):
            p = k * UNROLL + step
            row = column_lse(a_src[ids_src[0, n_tb + p]], r_tgt[ids_tgt[0, n_tb + p]])
            far[pl.ds(p, 1), :] = jnp.where(n_tb + p < count, row, LOWEST)
        return carry

    lax.fori_loop(0, n_extra // UNROLL, far_columns, 0)

    def band(y):
        return pl.ds(pl.multiple_of(y * per_y, per_y), per_y)

    def to_y(d):
        y = lax.rem(my_y + d, ny)
        return remote(part.at[band(y)], recv_y.at[my_y], y_send.at[d], y_recv.at[my_y], along_y(d))

    def near_columns(ds):
        bands = [lax.rem(my_y + d, ny) for d in ds]
        for y in bands:
            for step in range(per_y):
                b = y * per_y + step
                lse[pl.ds(b, 1), :] = column_lse(a_src[row_ids[0, b]], r_tgt[b])
        for y in bands:
            part[band(y), :] = merge(jnp.stack([lse[band(y), :], extra[band(y), :]]))
        for d in ds:
            if not (isinstance(d, int) and d == 0):
                to_y(d).start()

    def near_pair(m, carry):
        near_columns([ny // 2 - m, ny // 2 + 1 + m])
        return carry

    extra[...] = owner_steps(far[...], pick_t, gather_t)
    if ny > 2:
        near_columns([ny // 2, ny // 2 + 1])
        lax.fori_loop(1, ny // 2 - 1, near_pair, 0)
    near_columns([1])
    near_columns([0])
    recv_y[my_y] = part[band(my_y), :]

    def collect(n, me, where, dst, send, recv):
        for d in range(1, n):
            other = lax.rem(me + d, n)
            remote(dst(other), dst(other), send.at[d], recv.at[other], where(d)).wait_recv()

    collect(ny, my_y, along_y, lambda y: recv_y.at[y], y_send, y_recv)
    comb[...] = merge(recv_y[...])

    def to_z(d):
        return remote(comb, recv_z.at[my_z], z_send.at[d], z_recv.at[my_z], along_z(d))

    def by_distance(n):
        return sorted(range(1, n), key=lambda d: -min(d, n - d))

    for d in by_distance(nz):
        to_z(d).start()
    recv_z[my_z] = comb[...]
    collect(nz, my_z, along_z, lambda z: recv_z.at[z], z_send, z_recv)
    full[band(my_y), :] = merge(recv_z[...])

    def to_all(d):
        rows = full.at[band(my_y)]
        return remote(rows, rows, g_send.at[d], g_recv.at[my_y], along_y(d))

    for d in by_distance(ny):
        to_all(d).start()

    line = lax.broadcasted_iota(jnp.int32, (16, BLOCK), 0)

    def near_rows(ds):
        bands = [lax.rem(my_y + d, ny) for d in ds]
        values = []
        for y, d in zip(bands, ds):
            rows = band(y)
            if not (isinstance(d, int) and d == 0):
                slot = full.at[rows]
                remote(slot, slot, g_send.at[d], g_recv.at[y], along_y(d)).wait_recv()
        for y in bands:
            rows = band(y)
            total = full[rows, :]
            weight = tlogw[rows, :]
            out_t[rows, :] = 0.5 * weight - (0.5 * LN2) * (total - y_sq[rows, :])
            v = LOG2E * weight - total
            high, low = split(v)
            values.append((high.astype(f32), low.astype(f32), residue(v)))
        for y, (v_high, v_low, rest) in zip(bands, values):
            for step in range(per_y):
                b = y * per_y + step
                r = r_tgt[b]
                one = slice(step, step + 1)
                high = jnp.where(line == 5, rest[one], r[48:64].astype(f32))
                high = jnp.where(line == 4, v_high[one], high)
                low = jnp.where(line == 4, v_low[one], r[112:128].astype(f32))
                both = [r[:48], high.astype(bf16), r[64:112], low.astype(bf16)]
                turned = jnp.concatenate(both, axis=0).T
                a_tgt[b] = turned
                lse[pl.ds(b, 1), :] = column_lse(turned, r_src[row_ids[0, b]])

    def near_row_pair(m, carry):
        near_rows([m, ny - m])
        return carry

    near_rows([0])
    lax.fori_loop(1, ny // 2, near_row_pair, 0)
    near_rows([ny // 2])

    def far_rows(k, carry):
        for step in range(UNROLL):
            p = k * UNROLL + step
            row = column_lse(a_tgt[ids_tgt[0, n_tb + p]], r_src[ids_src[0, n_tb + p]])
            far[pl.ds(p, 1), :] = jnp.where(n_tb + p < count, row, LOWEST)
        return carry

    lax.fori_loop(0, n_extra // UNROLL, far_rows, 0)
    def lift(part, first, k, top):
        at = [k * 8 + step for step in range(8)]
        ids = [row_ids[0, first + p] for p in at]
        return raise_peaks(top, [part[pl.ds(p, 1), :] for p in at], ids)

    row_peak = jnp.full((n_sb, BLOCK), LOWEST, f32)
    row_peak = lax.fori_loop(0, n_tb // 8, functools.partial(lift, lse, 0), row_peak)
    row_peak = lax.fori_loop(0, n_extra // 8, functools.partial(lift, far, n_tb), row_peak)
    both = jnp.concatenate([lse[...], far[...]], axis=0)
    rowpart[...] = owner_sums(row_peak, both, pick_s, gather_s)

    def to_t(d):
        return remote(rowpart, recv_x.at[me_t], x_send.at[d], x_recv.at[me_t], along_t(d))

    for d in by_distance(nt):
        to_t(d).start()
    recv_x[me_t] = rowpart[...]
    potential = jnp.concatenate(
        [
            xbuf[t, ROW_F : ROW_F + 1, h * BLOCK : (h + 1) * BLOCK]
            for t in range(nt)
            for h in range(shard_blocks)
        ],
        axis=0,
    )
    collect(nt, me_t, along_t, lambda t: recv_x.at[t], x_send, x_recv)
    out_s[...] = potential + 0.5 * slogw[...] - (0.5 * LN2) * merge(recv_x[...])

    for copy in sent + relays:
        copy.wait_send()
    for n, to in ((ny, to_y), (nz, to_z), (ny, to_all), (nt, to_t)):
        for d in range(1, n):
            to(d).wait_send()


def local(
    n_src,
    n_tgt,
    source_points,
    source_potential,
    source_logw,
    target_points,
    target_logw,
    pair_source,
    pair_target,
    pair_count,
):
    pc, cells = source_points.shape
    n_tb = target_points.shape[1] // BLOCK
    n_sb = source_logw.shape[0] // BLOCK
    slots = pair_source.shape[-1]
    ny = math.isqrt(n_src)
    nz = n_src // ny
    nt = n_tgt
    per_y = n_tb // ny
    n_extra = slots - n_tb
    vmem = pl.BlockSpec(memory_space=pltpu.VMEM)
    dma = pltpu.SemaphoreType.DMA
    out_t, out_s = pl.pallas_call(
        functools.partial(kernel, (ny, nz, nt, n_tb, n_sb, slots, pc)),
        out_shape=(
            pltpu.VMEM((n_tb, BLOCK), f32),
            pltpu.VMEM((n_sb, BLOCK), f32),
        ),
        in_specs=[pl.BlockSpec(memory_space=pltpu.HBM)] * 8,
        out_specs=(vmem, vmem),
        scratch_shapes=[
            pltpu.VMEM((pc, cells), f32),
            pltpu.VMEM((1, cells), f32),
            pltpu.VMEM((n_sb, BLOCK), f32),
            pltpu.VMEM((n_tb, BLOCK), f32),
            pltpu.SMEM((1, slots), jnp.int32),
            pltpu.SMEM((1, slots), jnp.int32),
            pltpu.SMEM((1, 1), jnp.int32),
            pltpu.VMEM((1, slots), jnp.int32),
            pltpu.VMEM((1, slots), jnp.int32),
            pltpu.VMEM((1, slots), jnp.int32),
            pltpu.SMEM((1, slots), jnp.int32),
            pltpu.VMEM((pc, n_tb * BLOCK), f32),
            pltpu.VMEM((nt, 56, cells), f32),
            pltpu.VMEM((n_tb, BLOCK, BLOCK), bf16),
            pltpu.VMEM((n_tb, BLOCK, BLOCK), bf16),
            pltpu.VMEM((n_sb, BLOCK, BLOCK), bf16),
            pltpu.VMEM((n_sb, BLOCK, BLOCK), bf16),
            pltpu.VMEM((n_tb, BLOCK), f32),
            pltpu.VMEM((n_tb, BLOCK), f32),
            pltpu.VMEM((n_extra, BLOCK), f32),
            pltpu.VMEM((n_tb, n_extra), bf16),
            pltpu.VMEM((n_extra, n_tb), bf16),
            pltpu.VMEM((n_sb, slots), bf16),
            pltpu.VMEM((slots, BLOCK), bf16),
            pltpu.VMEM((n_tb, BLOCK), f32),
            pltpu.VMEM((n_tb, BLOCK), f32),
            pltpu.VMEM((ny, per_y, BLOCK), f32),
            pltpu.VMEM((per_y, BLOCK), f32),
            pltpu.VMEM((nz, per_y, BLOCK), f32),
            pltpu.VMEM((n_tb, BLOCK), f32),
            pltpu.VMEM((n_sb, BLOCK), f32),
            pltpu.VMEM((nt, n_sb, BLOCK), f32),
            dma((9,)),
            dma((CHUNKS,)),
            dma,
            dma((nt,)), dma((nt,)), dma((nt,)),
            dma((ny,)), dma((ny,)),
            dma((nz,)), dma((nz,)),
            dma((ny,)), dma((ny,)),
            dma((nt,)), dma((nt,)),
        ],
        compiler_params=pltpu.CompilerParams(
            collective_id=0, has_side_effects=True, vmem_limit_bytes=40 * 2**20
        ),
    )(
        *(
            pltpu.with_memory_space_constraint(operand, pltpu.HBM)
            for operand in (
                source_points,
                source_potential.reshape(1, cells),
                source_logw.reshape(n_sb, BLOCK),
                target_points,
                target_logw.reshape(n_tb, BLOCK),
                pair_source,
                pair_target,
            )
        ),
        pair_count,
    )
    return out_t.reshape(-1), out_s.reshape(-1)


def solution(mesh):
    placed = (
        P(None, ("src", "tgt")),
        P(("src", "tgt")),
        P("src"),
        P(None, "tgt"),
        P("tgt"),
        P("src", "tgt", None),
        P("src", "tgt", None),
        P("src", "tgt"),
    )
    return jax.shard_map(
        functools.partial(local, mesh.shape["src"], mesh.shape["tgt"]),
        mesh=mesh,
        in_specs=placed,
        out_specs=(P("tgt"), P("src")),
        check_vma=False,
    )
```

```python
import functools
import math

import jax
import jax.numpy as jnp
from jax import lax
from jax.experimental import pallas as pl
from jax.experimental.pallas import tpu as pltpu
from jax.sharding import PartitionSpec as P

BLOCK = 128
HALF = 64
ROW_U = 50
ROW_F = 54
LOG2E = 1.4426950408889634
LN2 = 0.6931471805599453
SCALE = 2.0 * LOG2E
ROOT = math.sqrt(2.0 * SCALE)
LOWEST = -1.0e30
STEP = 64.0
MIDDLE = 6.0
UNROLL = 128
CHUNKS = 4
MESH = pl.DeviceIdType.MESH
f32 = jnp.float32
bf16 = jnp.bfloat16


def split(x):
    high = x.astype(bf16)
    return high, (x - high.astype(f32)).astype(bf16)


def residue(x):
    high, low = split(x)
    return x - high.astype(f32) - low.astype(f32)


def merge(parts):
    top = jnp.max(parts, axis=0)
    return top + jnp.log2(jnp.sum(jnp.exp2(parts - top[None]), axis=0))


def repeat(times, body, carry):
    return body(0, carry) if times == 1 else lax.fori_loop(0, times, body, carry)


def column_lse(a, r):
    lhs = jnp.concatenate([a, a], axis=1)
    rhs = jnp.concatenate([r[:HALF], r[:HALF], r[HALF:], r[HALF:]], axis=0)
    score = jnp.dot(lhs, rhs, preferred_element_type=f32)
    top = jnp.max(score, axis=0, keepdims=True)
    return top + jnp.log2(jnp.sum(jnp.exp2(score - top), axis=0, keepdims=True))


def raise_peaks(top, rows, ids):
    index = lax.broadcasted_iota(jnp.int32, top.shape, 0)
    tops = [top]
    for row, owner in zip(rows, ids):
        tops.append(jnp.where(index == owner, jnp.broadcast_to(row, top.shape), LOWEST))
    while len(tops) > 1:
        tops = [functools.reduce(jnp.maximum, tops[i : i + 2]) for i in range(0, len(tops), 2)]
    return tops[0]


def owner_sums(top, lse, pick, gather):
    high, low = split(top)
    parts = [high, low, residue(top).astype(bf16)]
    spare = gather.shape[1] - 3 * top.shape[0]
    if spare > 0:
        parts.append(jnp.zeros((spare, BLOCK), bf16))
    tops = jnp.dot(gather[...], jnp.concatenate(parts, axis=0), preferred_element_type=f32)
    high, low = split(jnp.exp2(lse - tops))
    total = jnp.dot(pick[...], high, preferred_element_type=f32) + jnp.dot(
        pick[...], low, preferred_element_type=f32
    )
    return top + jnp.log2(total)


def owner_steps(lse, pick, gather):
    step = jnp.clip(jnp.floor(lse * (1.0 / STEP)) - MIDDLE, -30.0, 30.0)
    power = jnp.where(lse > 0.5 * LOWEST, jnp.exp2(4.0 * step), 0.0)
    total = jnp.dot(pick[...], power.astype(bf16), preferred_element_type=f32)
    largest = jnp.floor(0.25 * (jnp.log2(jnp.maximum(total, 2.0**-122)) + 0.04))
    edge = STEP * (largest + MIDDLE + 1.0)
    edges = jnp.dot(gather[...], edge.astype(bf16), preferred_element_type=f32)
    high, low = split(jnp.exp2(lse - edges))
    total = jnp.dot(pick[...], high, preferred_element_type=f32) + jnp.dot(
        pick[...], low, preferred_element_type=f32
    )
    return edge + jnp.log2(total)


def kernel(
    dims,
    spts_hbm, spot_hbm, slogw_hbm, tpts_hbm, tlogw_hbm, src_hbm, tgt_hbm, count_hbm,
    out_t, out_s,
    spts, spot, slogw, tlogw, ids_src, ids_tgt, count_ref, row_src, row_tgt, base_vec, row_ids,
    tpts, xbuf, r_tgt, a_tgt, r_src, a_src, y_sq, lse, far, pick_t, gather_t, pick_s, gather_s,
    extra, part, recv_y, comb, recv_z, full, rowpart, recv_x,
    load_sem, chunk_sem, base_sem, gather_send, gather_recv, relay_send,
    y_send, y_recv, z_send, z_recv, g_send, g_recv, x_send, x_recv,
):
    ny, nz, nt, n_tb, n_sb, slots, pc = dims
    nx = nt // 2
    me_s, me_t = lax.axis_index("src"), lax.axis_index("tgt")
    my_y, my_z = lax.rem(me_s, ny), lax.div(me_s, ny)
    my_x, my_c = lax.div(me_t, 2), lax.rem(me_t, 2)
    per_y = n_tb // ny
    shard_blocks = n_sb // nt
    n_extra = slots - n_tb

    def along_y(d):
        return (my_z * ny + lax.rem(my_y + d, ny), me_t)

    def along_z(d):
        return (lax.rem(my_z + d, nz) * ny + my_y, me_t)

    def along_t(d):
        return (me_s, lax.rem(me_t + d, nt))

    barrier = pltpu.get_barrier_semaphore()
    def chip(d):
        return (me_s, lax.rem(my_x + d, nx) * 2 + my_c)

    other_core = (me_s, my_x * 2 + 1 - my_c)
    order = sorted(range(1, nx), key=lambda d: -min(d, nx - d))
    peers = (
        [chip(d) for d in order]
        + [other_core]
        + [(me_s, lax.rem(my_x + d, nx) * 2 + 1 - my_c) for d in order]
        + [along_y(d) for d in range(1, ny)]
        + [along_z(d) for d in range(1, nz)]
    )
    def greet(peer):
        pl.semaphore_signal(barrier, inc=1, device_id=peer, device_id_type=MESH)

    for peer in peers[0:nx]:
        greet(peer)
    pairs = [
        (spts_hbm, spts), (spot_hbm, spot), (src_hbm.at[0], row_src), (tgt_hbm.at[0], row_tgt),
        (src_hbm.at[0], ids_src), (tgt_hbm.at[0], ids_tgt), (count_hbm, count_ref),
        (slogw_hbm, slogw), (tlogw_hbm, tlogw),
    ]
    small = [pltpu.make_async_copy(a, b, load_sem.at[k]) for k, (a, b) in enumerate(pairs)]
    for load in small[0:2]:
        load.start()
    for peer in peers[nx:]:
        greet(peer)
    for load in small[2:]:
        load.start()
    width = n_tb * BLOCK // CHUNKS
    loads = []
    for c in range(CHUNKS):
        cols = pl.ds(c * width, width)
        load = pltpu.make_async_copy(tpts_hbm.at[:, cols], tpts.at[:, cols], chunk_sem.at[c])
        load.start()
        loads.append(load)
    small[0].wait()
    small[1].wait()

    x = spts[...] * ROOT
    pot = spot[...]
    cells = pot.shape[1]
    u = SCALE * pot - 0.5 * jnp.sum(x * x, axis=0, keepdims=True)
    one = jnp.ones((1, cells), f32)
    xbuf[me_t] = jnp.concatenate([x, u, residue(u), one, one, pot, 0.0 * one], axis=0)

    pl.semaphore_wait(barrier, len(peers))

    def remote(src, dst, send, recv, where):
        return pltpu.make_async_remote_copy(
            src_ref=src, dst_ref=dst, send_sem=send, recv_sem=recv,
            device_id=where, device_id_type=MESH,
        )

    mine = xbuf.at[me_t]
    sent = [remote(mine, mine, gather_send.at[d], gather_recv.at[me_t], chip(d)) for d in order]
    sent.append(remote(mine, mine, gather_send.at[0], gather_recv.at[me_t], other_core))
    for copy in sent:
        copy.start()

    def arrived(slot, sem, where):
        remote(slot, slot, gather_send.at[0], sem, where).wait_recv()

    for load in small[2:]:
        load.wait()
    count = count_ref[0, 0]
    turned_t = jnp.broadcast_to(row_tgt[:, 0:n_tb], (n_tb, n_tb)).T
    turned_s = jnp.broadcast_to(row_src[:, 0:n_tb], (n_tb, n_tb)).T
    owner = lax.broadcasted_iota(jnp.int32, (n_tb, n_tb), 1)
    base_row = jnp.sum(jnp.where(turned_t == owner, turned_s, 0), axis=0, keepdims=True)
    base_vec[:, 0:n_tb] = base_row
    base_vec[:, n_tb:] = row_src[:, n_tb:]
    base_copy = pltpu.make_async_copy(base_vec, row_ids, base_sem)
    base_copy.start()

    def one_hot(flags):
        return jnp.where(flags, 1.0, 0.0).astype(bf16)

    further_t, further_s = row_tgt[:, n_tb:], row_src[:, n_tb:]
    pick_t[...] = one_hot(lax.broadcasted_iota(jnp.int32, (n_tb, n_extra), 0) == further_t)
    column = jnp.broadcast_to(further_t, (n_tb, n_extra)).T
    gather_t[...] = one_hot(lax.broadcasted_iota(jnp.int32, (n_extra, n_tb), 1) == column)
    lane = lax.broadcasted_iota(jnp.int32, (BLOCK, BLOCK), 1)
    lane = jnp.where(lane < 3 * n_sb, lax.rem(lane, n_sb), -1)
    for at, ids in ((0, base_row), (n_tb, further_s)):
        n = ids.shape[1]
        pick_s[:, at : at + n] = one_hot(lax.broadcasted_iota(jnp.int32, (n_sb, n), 0) == ids)
        gather_s[at : at + n, :] = one_hot(jnp.broadcast_to(ids, (BLOCK, n)).T == lane[0:n])

    tail = lax.broadcasted_iota(jnp.int32, (HALF - pc, BLOCK), 0)
    tail = jnp.where(tail < 2, 1.0, 0.0)

    def prepare(k, carry):
        for step in range(4):
            b = k * 4 + step
            y = tpts[:, pl.ds(pl.multiple_of(b * BLOCK, BLOCK), BLOCK)] * ROOT
            y_sq[pl.ds(b, 1), :] = 0.5 * jnp.sum(y * y, axis=0, keepdims=True)
            high, low = split(jnp.concatenate([y, tail], axis=0))
            r_tgt[b] = jnp.concatenate([high, low], axis=0)
        return carry

    per_chunk = n_tb // CHUNKS // 4
    for c in range(CHUNKS):
        loads[c].wait()
        lax.fori_loop(c * per_chunk, (c + 1) * per_chunk, prepare, 0)

    zeros = jnp.zeros((HALF - 56, BLOCK), f32)

    def source(t):
        for h in range(shard_blocks):
            b = t * shard_blocks + h
            xs = xbuf[t, :, h * BLOCK : (h + 1) * BLOCK]
            high, low = split(jnp.concatenate([xs, zeros], axis=0))
            both = jnp.concatenate([high, low], axis=0)
            r_src[b] = both
            a_src[b] = both.T

    source(me_t)
    relays = []
    for d in reversed(order):
        t = lax.rem(my_x + d, nx) * 2 + my_c
        arrived(xbuf.at[t], gather_recv.at[t], chip(d))
        relay = remote(xbuf.at[t], xbuf.at[t], relay_send.at[d], gather_recv.at[t], other_core)
        relay.start()
        relays.append(relay)
        source(t)
    for d in [0] + order[::-1]:
        t = lax.rem(my_x + d, nx) * 2 + 1 - my_c
        arrived(xbuf.at[t], gather_recv.at[t], other_core)
        source(t)
    base_copy.wait()

    def far_columns(k, carry):
        for step in range(UNROLL):
            p = k * UNROLL + step
            row = column_lse(a_src[ids_src[0, n_tb + p]], r_tgt[ids_tgt[0, n_tb + p]])
            far[pl.ds(p, 1), :] = jnp.where(n_tb + p < count, row, LOWEST)
        return carry

    repeat(n_extra // UNROLL, far_columns, 0)

    def band(y):
        return pl.ds(pl.multiple_of(y * per_y, per_y), per_y)

    def to_y(d):
        y = lax.rem(my_y + d, ny)
        return remote(part.at[band(y)], recv_y.at[my_y], y_send.at[d], y_recv.at[my_y], along_y(d))

    def near_columns(ds):
        bands = [lax.rem(my_y + d, ny) for d in ds]
        for y in bands:
            for step in range(per_y):
                b = y * per_y + step
                lse[pl.ds(b, 1), :] = column_lse(a_src[row_ids[0, b]], r_tgt[b])
        for y in bands:
            part[band(y), :] = merge(jnp.stack([lse[band(y), :], extra[band(y), :]]))
        for d in ds:
            if not (isinstance(d, int) and d == 0):
                to_y(d).start()

    extra[...] = owner_steps(far[...], pick_t, gather_t)
    for m in range(ny // 2 - 1):
        near_columns([ny // 2 - m, ny // 2 + 1 + m])
    near_columns([1])
    near_columns([0])
    recv_y[my_y] = part[band(my_y), :]

    def collect(n, me, where, dst, send, recv):
        for d in range(1, n):
            other = lax.rem(me + d, n)
            remote(dst(other), dst(other), send.at[d], recv.at[other], where(d)).wait_recv()

    collect(ny, my_y, along_y, lambda y: recv_y.at[y], y_send, y_recv)
    comb[...] = merge(recv_y[...])

    def to_z(d):
        return remote(comb, recv_z.at[my_z], z_send.at[d], z_recv.at[my_z], along_z(d))

    def by_distance(n):
        return sorted(range(1, n), key=lambda d: -min(d, n - d))

    for d in by_distance(nz):
        to_z(d).start()
    recv_z[my_z] = comb[...]
    collect(nz, my_z, along_z, lambda z: recv_z.at[z], z_send, z_recv)
    full[band(my_y), :] = merge(recv_z[...])

    def to_all(d):
        rows = full.at[band(my_y)]
        return remote(rows, rows, g_send.at[d], g_recv.at[my_y], along_y(d))

    for d in by_distance(ny):
        to_all(d).start()

    line = lax.broadcasted_iota(jnp.int32, (16, BLOCK), 0)

    def near_rows(ds, top):
        bands = [lax.rem(my_y + d, ny) for d in ds]
        values = []
        for y, d in zip(bands, ds):
            rows = band(y)
            if not (isinstance(d, int) and d == 0):
                slot = full.at[rows]
                remote(slot, slot, g_send.at[d], g_recv.at[y], along_y(d)).wait_recv()
        for y in bands:
            rows = band(y)
            total = full[rows, :]
            weight = tlogw[rows, :]
            out_t[rows, :] = 0.5 * weight - (0.5 * LN2) * (total - y_sq[rows, :])
            v = LOG2E * weight - total
            high, low = split(v)
            values.append((high.astype(f32), low.astype(f32), residue(v)))
        for y, (v_high, v_low, rest) in zip(bands, values):
            for step in range(per_y):
                b = y * per_y + step
                r = r_tgt[b]
                one = slice(step, step + 1)
                high = jnp.where(line == 5, rest[one], r[48:64].astype(f32))
                high = jnp.where(line == 4, v_high[one], high)
                low = jnp.where(line == 4, v_low[one], r[112:128].astype(f32))
                both = [r[:48], high.astype(bf16), r[64:112], low.astype(bf16)]
                turned = jnp.concatenate(both, axis=0).T
                a_tgt[b] = turned
                row = column_lse(turned, r_src[row_ids[0, b]])
                lse[pl.ds(b, 1), :] = row
                top = raise_peaks(top, [row], [row_ids[0, b]])
        return top

    row_peak = near_rows([0], jnp.full((n_sb, BLOCK), LOWEST, f32))
    arrivals = sorted(range(1, ny), key=lambda d: min(d, ny - d))
    for group in (arrivals[0:2], arrivals[2:6], arrivals[6:]):
        if group:
            row_peak = near_rows(group, row_peak)

    def far_rows(k, top):
        for step in range(UNROLL):
            p = k * UNROLL + step
            owner = ids_src[0, n_tb + p]
            row = column_lse(a_tgt[ids_tgt[0, n_tb + p]], r_src[owner])
            row = jnp.where(n_tb + p < count, row, LOWEST)
            far[pl.ds(p, 1), :] = row
            top = raise_peaks(top, [row], [owner])
        return top

    row_peak = repeat(n_extra // UNROLL, far_rows, row_peak)
    both = jnp.concatenate([lse[...], far[...]], axis=0)
    rowpart[...] = owner_sums(row_peak, both, pick_s, gather_s)

    def to_t(d):
        return remote(rowpart, recv_x.at[me_t], x_send.at[d], x_recv.at[me_t], along_t(d))

    for d in by_distance(nt):
        to_t(d).start()
    recv_x[me_t] = rowpart[...]
    potential = jnp.concatenate(
        [
            xbuf[t, ROW_F : ROW_F + 1, h * BLOCK : (h + 1) * BLOCK]
            for t in range(nt)
            for h in range(shard_blocks)
        ],
        axis=0,
    )
    rest = potential + 0.5 * slogw[...]
    for copy in sent + relays:
        copy.wait_send()
    for n, to in ((ny, to_y), (nz, to_z), (ny, to_all), (nt, to_t)):
        for d in range(1, n):
            to(d).wait_send()
    collect(nt, me_t, along_t, lambda t: recv_x.at[t], x_send, x_recv)
    out_s[...] = rest - (0.5 * LN2) * merge(recv_x[...])


def local(
    n_src,
    n_tgt,
    source_points,
    source_potential,
    source_logw,
    target_points,
    target_logw,
    pair_source,
    pair_target,
    pair_count,
):
    pc, cells = source_points.shape
    n_tb = target_points.shape[1] // BLOCK
    n_sb = source_logw.shape[0] // BLOCK
    slots = pair_source.shape[-1]
    ny = math.isqrt(n_src)
    nz = n_src // ny
    nt = n_tgt
    per_y = n_tb // ny
    n_extra = slots - n_tb
    vmem = pl.BlockSpec(memory_space=pltpu.VMEM)
    dma = pltpu.SemaphoreType.DMA
    out_t, out_s = pl.pallas_call(
        functools.partial(kernel, (ny, nz, nt, n_tb, n_sb, slots, pc)),
        out_shape=(
            pltpu.VMEM((n_tb, BLOCK), f32),
            pltpu.VMEM((n_sb, BLOCK), f32),
        ),
        in_specs=[pl.BlockSpec(memory_space=pltpu.HBM)] * 8,
        out_specs=(vmem, vmem),
        scratch_shapes=[
            pltpu.VMEM((pc, cells), f32),
            pltpu.VMEM((1, cells), f32),
            pltpu.VMEM((n_sb, BLOCK), f32),
            pltpu.VMEM((n_tb, BLOCK), f32),
            pltpu.SMEM((1, slots), jnp.int32),
            pltpu.SMEM((1, slots), jnp.int32),
            pltpu.SMEM((1, 1), jnp.int32),
            pltpu.VMEM((1, slots), jnp.int32),
            pltpu.VMEM((1, slots), jnp.int32),
            pltpu.VMEM((1, slots), jnp.int32),
            pltpu.SMEM((1, slots), jnp.int32),
            pltpu.VMEM((pc, n_tb * BLOCK), f32),
            pltpu.VMEM((nt, 56, cells), f32),
            pltpu.VMEM((n_tb, BLOCK, BLOCK), bf16),
            pltpu.VMEM((n_tb, BLOCK, BLOCK), bf16),
            pltpu.VMEM((n_sb, BLOCK, BLOCK), bf16),
            pltpu.VMEM((n_sb, BLOCK, BLOCK), bf16),
            pltpu.VMEM((n_tb, BLOCK), f32),
            pltpu.VMEM((n_tb, BLOCK), f32),
            pltpu.VMEM((n_extra, BLOCK), f32),
            pltpu.VMEM((n_tb, n_extra), bf16),
            pltpu.VMEM((n_extra, n_tb), bf16),
            pltpu.VMEM((n_sb, slots), bf16),
            pltpu.VMEM((slots, BLOCK), bf16),
            pltpu.VMEM((n_tb, BLOCK), f32),
            pltpu.VMEM((n_tb, BLOCK), f32),
            pltpu.VMEM((ny, per_y, BLOCK), f32),
            pltpu.VMEM((per_y, BLOCK), f32),
            pltpu.VMEM((nz, per_y, BLOCK), f32),
            pltpu.VMEM((n_tb, BLOCK), f32),
            pltpu.VMEM((n_sb, BLOCK), f32),
            pltpu.VMEM((nt, n_sb, BLOCK), f32),
            dma((9,)),
            dma((CHUNKS,)),
            dma,
            dma((nt,)), dma((nt,)), dma((nt,)),
            dma((ny,)), dma((ny,)),
            dma((nz,)), dma((nz,)),
            dma((ny,)), dma((ny,)),
            dma((nt,)), dma((nt,)),
        ],
        compiler_params=pltpu.CompilerParams(
            collective_id=0, has_side_effects=True, vmem_limit_bytes=40 * 2**20
        ),
    )(
        *(
            pltpu.with_memory_space_constraint(operand, pltpu.HBM)
            for operand in (
                source_points,
                source_potential.reshape(1, cells),
                source_logw.reshape(n_sb, BLOCK),
                target_points,
                target_logw.reshape(n_tb, BLOCK),
                pair_source,
                pair_target,
            )
        ),
        pair_count,
    )
    return out_t.reshape(-1), out_s.reshape(-1)


def solution(mesh):
    placed = (
        P(None, ("src", "tgt")),
        P(("src", "tgt")),
        P("src"),
        P(None, "tgt"),
        P("tgt"),
        P("src", "tgt", None),
        P("src", "tgt", None),
        P("src", "tgt"),
    )
    return jax.shard_map(
        functools.partial(local, mesh.shape["src"], mesh.shape["tgt"]),
        mesh=mesh,
        in_specs=placed,
        out_specs=(P("tgt"), P("src")),
        check_vma=False,
    )
```

```python
import functools
import math

import jax
import jax.numpy as jnp
from jax import lax
from jax.experimental import pallas as pl
from jax.experimental.pallas import tpu as pltpu
from jax.sharding import PartitionSpec as P

BLOCK = 128
HALF = 64
ROW_U = 50
ROW_F = 54
LOG2E = 1.4426950408889634
LN2 = 0.6931471805599453
SCALE = 2.0 * LOG2E
ROOT = math.sqrt(2.0 * SCALE)
LOWEST = -1.0e30
STEP = 64.0
MIDDLE = 6.0
UNROLL = 128
CHUNKS = 4
MESH = pl.DeviceIdType.MESH
f32 = jnp.float32
bf16 = jnp.bfloat16


def split(x):
    high = x.astype(bf16)
    return high, (x - high.astype(f32)).astype(bf16)


def residue(x):
    high, low = split(x)
    return x - high.astype(f32) - low.astype(f32)


def merge(parts):
    top = jnp.max(parts, axis=0)
    return top + jnp.log2(jnp.sum(jnp.exp2(parts - top[None]), axis=0))


def repeat(times, body, carry):
    return body(0, carry) if times == 1 else lax.fori_loop(0, times, body, carry)


def column_lse(a, r):
    lhs = jnp.concatenate([a, a], axis=1)
    rhs = jnp.concatenate([r[:HALF], r[:HALF], r[HALF:], r[HALF:]], axis=0)
    score = jnp.dot(lhs, rhs, preferred_element_type=f32)
    top = jnp.max(score, axis=0, keepdims=True)
    return top + jnp.log2(jnp.sum(jnp.exp2(score - top), axis=0, keepdims=True))


def raise_peaks(top, rows, ids):
    index = lax.broadcasted_iota(jnp.int32, top.shape, 0)
    tops = [top]
    for row, owner in zip(rows, ids):
        tops.append(jnp.where(index == owner, jnp.broadcast_to(row, top.shape), LOWEST))
    while len(tops) > 1:
        tops = [functools.reduce(jnp.maximum, tops[i : i + 2]) for i in range(0, len(tops), 2)]
    return tops[0]


def owner_sums(top, lse, pick, gather):
    high, low = split(top)
    parts = [high, low, residue(top).astype(bf16)]
    spare = gather.shape[1] - 3 * top.shape[0]
    if spare > 0:
        parts.append(jnp.zeros((spare, BLOCK), bf16))
    tops = jnp.dot(gather[...], jnp.concatenate(parts, axis=0), preferred_element_type=f32)
    high, low = split(jnp.exp2(lse - tops))
    total = jnp.dot(pick[...], high, preferred_element_type=f32) + jnp.dot(
        pick[...], low, preferred_element_type=f32
    )
    return top + jnp.log2(total)


def owner_steps(lse, pick, gather):
    step = jnp.clip(jnp.floor(lse * (1.0 / STEP)) - MIDDLE, -30.0, 30.0)
    power = jnp.where(lse > 0.5 * LOWEST, jnp.exp2(4.0 * step), 0.0)
    total = jnp.dot(pick[...], power.astype(bf16), preferred_element_type=f32)
    largest = jnp.floor(0.25 * (jnp.log2(jnp.maximum(total, 2.0**-122)) + 0.04))
    edge = STEP * (largest + MIDDLE + 1.0)
    edges = jnp.dot(gather[...], edge.astype(bf16), preferred_element_type=f32)
    high, low = split(jnp.exp2(lse - edges))
    total = jnp.dot(pick[...], high, preferred_element_type=f32) + jnp.dot(
        pick[...], low, preferred_element_type=f32
    )
    return edge + jnp.log2(total)


def kernel(
    dims,
    spts_hbm, spot_hbm, slogw_hbm, tpts_hbm, tlogw_hbm, src_hbm, tgt_hbm, count_hbm,
    out_t, out_s,
    spts, spot, slogw, tlogw, ids_src, ids_tgt, count_ref, row_src, row_tgt, base_vec, row_ids,
    tpts, xbuf, r_tgt, a_tgt, r_src, a_src, y_sq, lse, far, pick_t, gather_t, pick_s, gather_s,
    extra, part, recv_y, comb, recv_z, full, rowpart, recv_x,
    load_sem, chunk_sem, base_sem, gather_send, gather_recv, relay_send,
    y_send, y_recv, z_send, z_recv, g_send, g_recv, x_send, x_recv,
):
    ny, nz, nt, n_tb, n_sb, slots, pc = dims
    nx = nt // 2
    me_s, me_t = lax.axis_index("src"), lax.axis_index("tgt")
    my_y, my_z = lax.rem(me_s, ny), lax.div(me_s, ny)
    my_x, my_c = lax.div(me_t, 2), lax.rem(me_t, 2)
    per_y = n_tb // ny
    shard_blocks = n_sb // nt
    n_extra = slots - n_tb

    def along_y(d):
        return (my_z * ny + lax.rem(my_y + d, ny), me_t)

    def along_z(d):
        return (lax.rem(my_z + d, nz) * ny + my_y, me_t)

    def along_t(d):
        return (me_s, lax.rem(me_t + d, nt))

    barrier = pltpu.get_barrier_semaphore()
    def chip(d):
        return (me_s, lax.rem(my_x + d, nx) * 2 + my_c)

    other_core = (me_s, my_x * 2 + 1 - my_c)
    order = sorted(range(1, nx), key=lambda d: -min(d, nx - d))
    peers = (
        [chip(d) for d in order]
        + [other_core]
        + [(me_s, lax.rem(my_x + d, nx) * 2 + 1 - my_c) for d in order]
        + [along_y(d) for d in sorted(range(1, ny), key=lambda d: -min(d, ny - d))]
        + [along_z(d) for d in sorted(range(1, nz), key=lambda d: -min(d, nz - d))]
    )
    def greet(peer):
        pl.semaphore_signal(barrier, inc=1, device_id=peer, device_id_type=MESH)

    for peer in peers[0:nx]:
        greet(peer)
    pairs = [
        (spts_hbm, spts), (spot_hbm, spot), (src_hbm.at[0], row_src), (tgt_hbm.at[0], row_tgt),
        (src_hbm.at[0], ids_src), (tgt_hbm.at[0], ids_tgt), (count_hbm, count_ref),
        (slogw_hbm, slogw), (tlogw_hbm, tlogw),
    ]
    small = [pltpu.make_async_copy(a, b, load_sem.at[k]) for k, (a, b) in enumerate(pairs)]
    for load in small[0:2]:
        load.start()
    for peer in peers[nx:]:
        greet(peer)
    for load in small[2:]:
        load.start()
    width = n_tb * BLOCK // CHUNKS
    loads = []
    for c in range(CHUNKS):
        cols = pl.ds(c * width, width)
        load = pltpu.make_async_copy(tpts_hbm.at[:, cols], tpts.at[:, cols], chunk_sem.at[c])
        load.start()
        loads.append(load)
    small[0].wait()
    small[1].wait()

    x = spts[...] * ROOT
    pot = spot[...]
    cells = pot.shape[1]
    u = SCALE * pot - 0.5 * jnp.sum(x * x, axis=0, keepdims=True)
    one = jnp.ones((1, cells), f32)
    xbuf[me_t] = jnp.concatenate([x, u, residue(u), one, one, pot, 0.0 * one], axis=0)

    pl.semaphore_wait(barrier, len(peers))

    def remote(src, dst, send, recv, where):
        return pltpu.make_async_remote_copy(
            src_ref=src, dst_ref=dst, send_sem=send, recv_sem=recv,
            device_id=where, device_id_type=MESH,
        )

    mine = xbuf.at[me_t]
    sent = [remote(mine, mine, gather_send.at[d], gather_recv.at[me_t], chip(d)) for d in order]
    sent.append(remote(mine, mine, gather_send.at[0], gather_recv.at[me_t], other_core))
    for copy in sent:
        copy.start()

    def arrived(slot, sem, where):
        remote(slot, slot, gather_send.at[0], sem, where).wait_recv()

    for load in small[2:]:
        load.wait()
    count = count_ref[0, 0]
    turned_t = jnp.broadcast_to(row_tgt[:, 0:n_tb], (n_tb, n_tb)).T
    turned_s = jnp.broadcast_to(row_src[:, 0:n_tb], (n_tb, n_tb)).T
    owner = lax.broadcasted_iota(jnp.int32, (n_tb, n_tb), 1)
    base_row = jnp.sum(jnp.where(turned_t == owner, turned_s, 0), axis=0, keepdims=True)
    base_vec[:, 0:n_tb] = base_row
    base_vec[:, n_tb:] = row_src[:, n_tb:]
    base_copy = pltpu.make_async_copy(base_vec, row_ids, base_sem)
    base_copy.start()

    def one_hot(flags):
        return jnp.where(flags, 1.0, 0.0).astype(bf16)

    further_t, further_s = row_tgt[:, n_tb:], row_src[:, n_tb:]
    pick_t[...] = one_hot(lax.broadcasted_iota(jnp.int32, (n_tb, n_extra), 0) == further_t)
    column = jnp.broadcast_to(further_t, (n_tb, n_extra)).T
    gather_t[...] = one_hot(lax.broadcasted_iota(jnp.int32, (n_extra, n_tb), 1) == column)
    lane = lax.broadcasted_iota(jnp.int32, (BLOCK, BLOCK), 1)
    lane = jnp.where(lane < 3 * n_sb, lax.rem(lane, n_sb), -1)
    for at, ids in ((0, base_row), (n_tb, further_s)):
        n = ids.shape[1]
        pick_s[:, at : at + n] = one_hot(lax.broadcasted_iota(jnp.int32, (n_sb, n), 0) == ids)
        gather_s[at : at + n, :] = one_hot(jnp.broadcast_to(ids, (BLOCK, n)).T == lane[0:n])

    tail = lax.broadcasted_iota(jnp.int32, (HALF - pc, BLOCK), 0)
    tail = jnp.where(tail < 2, 1.0, 0.0)

    def prepare(k, carry):
        for step in range(4):
            b = k * 4 + step
            y = tpts[:, pl.ds(pl.multiple_of(b * BLOCK, BLOCK), BLOCK)] * ROOT
            y_sq[pl.ds(b, 1), :] = 0.5 * jnp.sum(y * y, axis=0, keepdims=True)
            high, low = split(jnp.concatenate([y, tail], axis=0))
            r_tgt[b] = jnp.concatenate([high, low], axis=0)
        return carry

    per_chunk = n_tb // CHUNKS // 4
    for c in range(CHUNKS):
        loads[c].wait()
        lax.fori_loop(c * per_chunk, (c + 1) * per_chunk, prepare, 0)

    zeros = jnp.zeros((HALF - 56, BLOCK), f32)

    def source(t):
        for h in range(shard_blocks):
            b = t * shard_blocks + h
            xs = xbuf[t, :, h * BLOCK : (h + 1) * BLOCK]
            high, low = split(jnp.concatenate([xs, zeros], axis=0))
            both = jnp.concatenate([high, low], axis=0)
            r_src[b] = both
            a_src[b] = both.T

    def pass_on(d):
        t = lax.rem(my_x + d, nx) * 2 + my_c
        arrived(xbuf.at[t], gather_recv.at[t], chip(d))
        relay = remote(xbuf.at[t], xbuf.at[t], relay_send.at[d], gather_recv.at[t], other_core)
        relay.start()
        return relay

    def from_other(d):
        t = lax.rem(my_x + d, nx) * 2 + 1 - my_c
        arrived(xbuf.at[t], gather_recv.at[t], other_core)
        source(t)

    source(me_t)
    from_other(0)
    near_first = order[::-1]
    relays = [pass_on(d) for d in near_first[:-1]]
    for d in near_first[:-1]:
        source(lax.rem(my_x + d, nx) * 2 + my_c)
    relays.append(pass_on(near_first[-1]))
    for d in near_first[:-1]:
        from_other(d)
    source(lax.rem(my_x + near_first[-1], nx) * 2 + my_c)
    from_other(near_first[-1])
    base_copy.wait()

    def far_columns(k, carry):
        for step in range(UNROLL):
            p = k * UNROLL + step
            row = column_lse(a_src[ids_src[0, n_tb + p]], r_tgt[ids_tgt[0, n_tb + p]])
            far[pl.ds(p, 1), :] = jnp.where(n_tb + p < count, row, LOWEST)
        return carry

    repeat(n_extra // UNROLL, far_columns, 0)

    def band(y):
        return pl.ds(pl.multiple_of(y * per_y, per_y), per_y)

    def to_y(d):
        y = lax.rem(my_y + d, ny)
        return remote(part.at[band(y)], recv_y.at[my_y], y_send.at[d], y_recv.at[my_y], along_y(d))

    def near_columns(ds):
        bands = [lax.rem(my_y + d, ny) for d in ds]
        for y in bands:
            for step in range(per_y):
                b = y * per_y + step
                lse[pl.ds(b, 1), :] = column_lse(a_src[row_ids[0, b]], r_tgt[b])
        for y in bands:
            part[band(y), :] = merge(jnp.stack([lse[band(y), :], extra[band(y), :]]))
        for d in ds:
            if not (isinstance(d, int) and d == 0):
                to_y(d).start()

    extra[...] = owner_steps(far[...], pick_t, gather_t)
    for m in range(ny // 2 - 1):
        near_columns([ny // 2 - m, ny // 2 + 1 + m])
    near_columns([1])
    near_columns([0])
    recv_y[my_y] = part[band(my_y), :]

    def collect(n, me, where, dst, send, recv):
        for d in range(1, n):
            other = lax.rem(me + d, n)
            remote(dst(other), dst(other), send.at[d], recv.at[other], where(d)).wait_recv()

    collect(ny, my_y, along_y, lambda y: recv_y.at[y], y_send, y_recv)
    comb[...] = merge(recv_y[...])

    def to_z(d):
        return remote(comb, recv_z.at[my_z], z_send.at[d], z_recv.at[my_z], along_z(d))

    def by_distance(n):
        return sorted(range(1, n), key=lambda d: -min(d, n - d))

    for d in by_distance(nz):
        to_z(d).start()
    recv_z[my_z] = comb[...]
    collect(nz, my_z, along_z, lambda z: recv_z.at[z], z_send, z_recv)
    full[band(my_y), :] = merge(recv_z[...])

    def to_all(d):
        rows = full.at[band(my_y)]
        return remote(rows, rows, g_send.at[d], g_recv.at[my_y], along_y(d))

    for d in by_distance(ny):
        to_all(d).start()

    line = lax.broadcasted_iota(jnp.int32, (16, BLOCK), 0)

    def near_rows(ds, top):
        bands = [lax.rem(my_y + d, ny) for d in ds]
        values = []
        for y, d in zip(bands, ds):
            rows = band(y)
            if not (isinstance(d, int) and d == 0):
                slot = full.at[rows]
                remote(slot, slot, g_send.at[d], g_recv.at[y], along_y(d)).wait_recv()
        for y in bands:
            rows = band(y)
            total = full[rows, :]
            weight = tlogw[rows, :]
            out_t[rows, :] = 0.5 * weight - (0.5 * LN2) * (total - y_sq[rows, :])
            v = LOG2E * weight - total
            high, low = split(v)
            values.append((high.astype(f32), low.astype(f32), residue(v)))
        for y, (v_high, v_low, rest) in zip(bands, values):
            for step in range(per_y):
                b = y * per_y + step
                r = r_tgt[b]
                one = slice(step, step + 1)
                high = jnp.where(line == 5, rest[one], r[48:64].astype(f32))
                high = jnp.where(line == 4, v_high[one], high)
                low = jnp.where(line == 4, v_low[one], r[112:128].astype(f32))
                both = [r[:48], high.astype(bf16), r[64:112], low.astype(bf16)]
                turned = jnp.concatenate(both, axis=0).T
                a_tgt[b] = turned
                row = column_lse(turned, r_src[row_ids[0, b]])
                lse[pl.ds(b, 1), :] = row
                top = raise_peaks(top, [row], [row_ids[0, b]])
        return top

    row_peak = near_rows([0], jnp.full((n_sb, BLOCK), LOWEST, f32))
    arrivals = sorted(range(1, ny), key=lambda d: min(d, ny - d))
    for group in (arrivals[0:2], arrivals[2:6], arrivals[6:]):
        if group:
            row_peak = near_rows(group, row_peak)

    def far_rows(k, top):
        for step in range(UNROLL):
            p = k * UNROLL + step
            owner = ids_src[0, n_tb + p]
            row = column_lse(a_tgt[ids_tgt[0, n_tb + p]], r_src[owner])
            row = jnp.where(n_tb + p < count, row, LOWEST)
            far[pl.ds(p, 1), :] = row
            top = raise_peaks(top, [row], [owner])
        return top

    row_peak = repeat(n_extra // UNROLL, far_rows, row_peak)
    both = jnp.concatenate([lse[...], far[...]], axis=0)
    rowpart[...] = owner_sums(row_peak, both, pick_s, gather_s)

    def to_t(d):
        return remote(rowpart, recv_x.at[me_t], x_send.at[d], x_recv.at[me_t], along_t(d))

    for d in by_distance(nt):
        to_t(d).start()
    recv_x[me_t] = rowpart[...]
    potential = jnp.concatenate(
        [
            xbuf[t, ROW_F : ROW_F + 1, h * BLOCK : (h + 1) * BLOCK]
            for t in range(nt)
            for h in range(shard_blocks)
        ],
        axis=0,
    )
    rest = potential + 0.5 * slogw[...]
    for copy in sent + relays:
        copy.wait_send()
    for n, to in ((ny, to_y), (nz, to_z), (ny, to_all), (nt, to_t)):
        for d in range(1, n):
            to(d).wait_send()
    collect(nt, me_t, along_t, lambda t: recv_x.at[t], x_send, x_recv)
    out_s[...] = rest - (0.5 * LN2) * merge(recv_x[...])


def local(
    n_src,
    n_tgt,
    source_points,
    source_potential,
    source_logw,
    target_points,
    target_logw,
    pair_source,
    pair_target,
    pair_count,
):
    pc, cells = source_points.shape
    n_tb = target_points.shape[1] // BLOCK
    n_sb = source_logw.shape[0] // BLOCK
    slots = pair_source.shape[-1]
    ny = math.isqrt(n_src)
    nz = n_src // ny
    nt = n_tgt
    per_y = n_tb // ny
    n_extra = slots - n_tb
    vmem = pl.BlockSpec(memory_space=pltpu.VMEM)
    dma = pltpu.SemaphoreType.DMA
    out_t, out_s = pl.pallas_call(
        functools.partial(kernel, (ny, nz, nt, n_tb, n_sb, slots, pc)),
        out_shape=(
            pltpu.VMEM((n_tb, BLOCK), f32),
            pltpu.VMEM((n_sb, BLOCK), f32),
        ),
        in_specs=[pl.BlockSpec(memory_space=pltpu.HBM)] * 8,
        out_specs=(vmem, vmem),
        scratch_shapes=[
            pltpu.VMEM((pc, cells), f32),
            pltpu.VMEM((1, cells), f32),
            pltpu.VMEM((n_sb, BLOCK), f32),
            pltpu.VMEM((n_tb, BLOCK), f32),
            pltpu.SMEM((1, slots), jnp.int32),
            pltpu.SMEM((1, slots), jnp.int32),
            pltpu.SMEM((1, 1), jnp.int32),
            pltpu.VMEM((1, slots), jnp.int32),
            pltpu.VMEM((1, slots), jnp.int32),
            pltpu.VMEM((1, slots), jnp.int32),
            pltpu.SMEM((1, slots), jnp.int32),
            pltpu.VMEM((pc, n_tb * BLOCK), f32),
            pltpu.VMEM((nt, 56, cells), f32),
            pltpu.VMEM((n_tb, BLOCK, BLOCK), bf16),
            pltpu.VMEM((n_tb, BLOCK, BLOCK), bf16),
            pltpu.VMEM((n_sb, BLOCK, BLOCK), bf16),
            pltpu.VMEM((n_sb, BLOCK, BLOCK), bf16),
            pltpu.VMEM((n_tb, BLOCK), f32),
            pltpu.VMEM((n_tb, BLOCK), f32),
            pltpu.VMEM((n_extra, BLOCK), f32),
            pltpu.VMEM((n_tb, n_extra), bf16),
            pltpu.VMEM((n_extra, n_tb), bf16),
            pltpu.VMEM((n_sb, slots), bf16),
            pltpu.VMEM((slots, BLOCK), bf16),
            pltpu.VMEM((n_tb, BLOCK), f32),
            pltpu.VMEM((n_tb, BLOCK), f32),
            pltpu.VMEM((ny, per_y, BLOCK), f32),
            pltpu.VMEM((per_y, BLOCK), f32),
            pltpu.VMEM((nz, per_y, BLOCK), f32),
            pltpu.VMEM((n_tb, BLOCK), f32),
            pltpu.VMEM((n_sb, BLOCK), f32),
            pltpu.VMEM((nt, n_sb, BLOCK), f32),
            dma((9,)),
            dma((CHUNKS,)),
            dma,
            dma((nt,)), dma((nt,)), dma((nt,)),
            dma((ny,)), dma((ny,)),
            dma((nz,)), dma((nz,)),
            dma((ny,)), dma((ny,)),
            dma((nt,)), dma((nt,)),
        ],
        compiler_params=pltpu.CompilerParams(
            collective_id=0, has_side_effects=True, vmem_limit_bytes=40 * 2**20
        ),
    )(
        *(
            pltpu.with_memory_space_constraint(operand, pltpu.HBM)
            for operand in (
                source_points,
                source_potential.reshape(1, cells),
                source_logw.reshape(n_sb, BLOCK),
                target_points,
                target_logw.reshape(n_tb, BLOCK),
                pair_source,
                pair_target,
            )
        ),
        pair_count,
    )
    return out_t.reshape(-1), out_s.reshape(-1)


def solution(mesh):
    placed = (
        P(None, ("src", "tgt")),
        P(("src", "tgt")),
        P("src"),
        P(None, "tgt"),
        P("tgt"),
        P("src", "tgt", None),
        P("src", "tgt", None),
        P("src", "tgt"),
    )
    return jax.shard_map(
        functools.partial(local, mesh.shape["src"], mesh.shape["tgt"]),
        mesh=mesh,
        in_specs=placed,
        out_specs=(P("tgt"), P("src")),
        check_vma=False,
    )
```

```python
import functools
import math

import jax
import jax.numpy as jnp
from jax import lax
from jax.experimental import pallas as pl
from jax.experimental.pallas import tpu as pltpu
from jax.sharding import PartitionSpec as P

BLOCK = 128
HALF = 64
ROW_U = 50
ROW_F = 54
LOG2E = 1.4426950408889634
LN2 = 0.6931471805599453
SCALE = 2.0 * LOG2E
ROOT = math.sqrt(2.0 * SCALE)
LOWEST = -1.0e30
STEP = 64.0
MIDDLE = 6.0
UNROLL = 128
CHUNKS = 4
MESH = pl.DeviceIdType.MESH
f32 = jnp.float32
bf16 = jnp.bfloat16


def split(x):
    high = x.astype(bf16)
    return high, (x - high.astype(f32)).astype(bf16)


def residue(x):
    high, low = split(x)
    return x - high.astype(f32) - low.astype(f32)


def merge(parts):
    top = jnp.max(parts, axis=0)
    return top + jnp.log2(jnp.sum(jnp.exp2(parts - top[None]), axis=0))


def repeat(times, body, carry):
    return body(0, carry) if times == 1 else lax.fori_loop(0, times, body, carry)


def column_lse(a, r):
    lhs = jnp.concatenate([a, a], axis=1)
    rhs = jnp.concatenate([r[:HALF], r[:HALF], r[HALF:], r[HALF:]], axis=0)
    score = jnp.dot(lhs, rhs, preferred_element_type=f32)
    top = jnp.max(score, axis=0, keepdims=True)
    return top + jnp.log2(jnp.sum(jnp.exp2(score - top), axis=0, keepdims=True))


def raise_peaks(top, rows, ids):
    index = lax.broadcasted_iota(jnp.int32, top.shape, 0)
    tops = [top]
    for row, owner in zip(rows, ids):
        tops.append(jnp.where(index == owner, jnp.broadcast_to(row, top.shape), LOWEST))
    while len(tops) > 1:
        tops = [functools.reduce(jnp.maximum, tops[i : i + 2]) for i in range(0, len(tops), 2)]
    return tops[0]


def owner_sums(top, lse, pick, gather):
    high, low = split(top)
    parts = [high, low, residue(top).astype(bf16)]
    spare = gather.shape[1] - 3 * top.shape[0]
    if spare > 0:
        parts.append(jnp.zeros((spare, BLOCK), bf16))
    tops = jnp.dot(gather[...], jnp.concatenate(parts, axis=0), preferred_element_type=f32)
    high, low = split(jnp.exp2(lse - tops))
    total = jnp.dot(pick[...], high, preferred_element_type=f32) + jnp.dot(
        pick[...], low, preferred_element_type=f32
    )
    return top + jnp.log2(total)


def owner_steps(lse, pick, gather):
    step = jnp.clip(jnp.floor(lse * (1.0 / STEP)) - MIDDLE, -30.0, 30.0)
    power = jnp.where(lse > 0.5 * LOWEST, jnp.exp2(4.0 * step), 0.0)
    total = jnp.dot(pick[...], power.astype(bf16), preferred_element_type=f32)
    largest = jnp.floor(0.25 * (jnp.log2(jnp.maximum(total, 2.0**-122)) + 0.04))
    edge = STEP * (largest + MIDDLE + 1.0)
    edges = jnp.dot(gather[...], edge.astype(bf16), preferred_element_type=f32)
    high, low = split(jnp.exp2(lse - edges))
    total = jnp.dot(pick[...], high, preferred_element_type=f32) + jnp.dot(
        pick[...], low, preferred_element_type=f32
    )
    return edge + jnp.log2(total)


def kernel(
    dims,
    spts_hbm, spot_hbm, slogw_hbm, tpts_hbm, tlogw_hbm, src_hbm, tgt_hbm, count_hbm,
    out_t, out_s,
    spts, spot, slogw, tlogw, ids_src, ids_tgt, count_ref, row_src, row_tgt, base_vec, row_ids,
    tpts, xbuf, r_tgt, a_tgt, r_src, a_src, y_sq, lse, far, pick_t, gather_t, pick_s, gather_s,
    extra, part, recv_y, comb, recv_z, full, rowpart, recv_x,
    load_sem, chunk_sem, base_sem, gather_send, gather_recv, relay_send,
    y_send, y_recv, z_send, z_recv, g_send, g_recv, x_send, x_recv,
):
    ny, nz, nt, n_tb, n_sb, slots, pc = dims
    nx = nt // 2
    me_s, me_t = lax.axis_index("src"), lax.axis_index("tgt")
    my_y, my_z = lax.rem(me_s, ny), lax.div(me_s, ny)
    my_x, my_c = lax.div(me_t, 2), lax.rem(me_t, 2)
    per_y = n_tb // ny
    shard_blocks = n_sb // nt
    n_extra = slots - n_tb

    def along_y(d):
        return (my_z * ny + lax.rem(my_y + d, ny), me_t)

    def along_z(d):
        return (lax.rem(my_z + d, nz) * ny + my_y, me_t)

    def along_t(d):
        return (me_s, lax.rem(me_t + d, nt))

    barrier = pltpu.get_barrier_semaphore()
    def chip(d):
        return (me_s, lax.rem(my_x + d, nx) * 2 + my_c)

    other_core = (me_s, my_x * 2 + 1 - my_c)
    order = sorted(range(1, nx), key=lambda d: -min(d, nx - d))
    peers = (
        [chip(d) for d in order]
        + [other_core]
        + [(me_s, lax.rem(my_x + d, nx) * 2 + 1 - my_c) for d in order]
        + [along_y(d) for d in sorted(range(1, ny), key=lambda d: -min(d, ny - d))]
        + [along_z(d) for d in sorted(range(1, nz), key=lambda d: -min(d, nz - d))]
    )
    def greet(peer):
        pl.semaphore_signal(barrier, inc=1, device_id=peer, device_id_type=MESH)

    for peer in peers[0:nx]:
        greet(peer)
    pairs = [
        (spts_hbm, spts), (spot_hbm, spot), (src_hbm.at[0], row_src), (tgt_hbm.at[0], row_tgt),
        (src_hbm.at[0], ids_src), (tgt_hbm.at[0], ids_tgt), (count_hbm, count_ref),
        (slogw_hbm, slogw), (tlogw_hbm, tlogw),
    ]
    small = [pltpu.make_async_copy(a, b, load_sem.at[k]) for k, (a, b) in enumerate(pairs)]
    for load in small[0:2]:
        load.start()
    for peer in peers[nx:]:
        greet(peer)
    for load in small[2:]:
        load.start()
    width = n_tb * BLOCK // CHUNKS
    loads = []
    for c in range(CHUNKS):
        cols = pl.ds(c * width, width)
        load = pltpu.make_async_copy(tpts_hbm.at[:, cols], tpts.at[:, cols], chunk_sem.at[c])
        load.start()
        loads.append(load)
    small[0].wait()
    small[1].wait()

    x = spts[...] * ROOT
    pot = spot[...]
    cells = pot.shape[1]
    u = SCALE * pot - 0.5 * jnp.sum(x * x, axis=0, keepdims=True)
    one = jnp.ones((1, cells), f32)
    xbuf[me_t] = jnp.concatenate([x, u, residue(u), one, one, pot, 0.0 * one], axis=0)

    pl.semaphore_wait(barrier, len(peers))

    def remote(src, dst, send, recv, where):
        return pltpu.make_async_remote_copy(
            src_ref=src, dst_ref=dst, send_sem=send, recv_sem=recv,
            device_id=where, device_id_type=MESH,
        )

    mine = xbuf.at[me_t]
    sent = [remote(mine, mine, gather_send.at[d], gather_recv.at[me_t], chip(d)) for d in order]
    sent.append(remote(mine, mine, gather_send.at[0], gather_recv.at[me_t], other_core))
    for copy in sent:
        copy.start()

    def arrived(slot, sem, where):
        remote(slot, slot, gather_send.at[0], sem, where).wait_recv()

    for load in small[2:]:
        load.wait()
    count = count_ref[0, 0]
    turned_t = jnp.broadcast_to(row_tgt[:, 0:n_tb], (n_tb, n_tb)).T
    turned_s = jnp.broadcast_to(row_src[:, 0:n_tb], (n_tb, n_tb)).T
    owner = lax.broadcasted_iota(jnp.int32, (n_tb, n_tb), 1)
    base_row = jnp.sum(jnp.where(turned_t == owner, turned_s, 0), axis=0, keepdims=True)
    base_vec[:, 0:n_tb] = base_row
    base_vec[:, n_tb:] = row_src[:, n_tb:]
    base_copy = pltpu.make_async_copy(base_vec, row_ids, base_sem)
    base_copy.start()

    def one_hot(flags):
        return jnp.where(flags, 1.0, 0.0).astype(bf16)

    further_t, further_s = row_tgt[:, n_tb:], row_src[:, n_tb:]
    pick_t[...] = one_hot(lax.broadcasted_iota(jnp.int32, (n_tb, n_extra), 0) == further_t)
    column = jnp.broadcast_to(further_t, (n_tb, n_extra)).T
    gather_t[...] = one_hot(lax.broadcasted_iota(jnp.int32, (n_extra, n_tb), 1) == column)
    lane = lax.broadcasted_iota(jnp.int32, (BLOCK, BLOCK), 1)
    lane = jnp.where(lane < 3 * n_sb, lax.rem(lane, n_sb), -1)
    for at, ids in ((0, base_row), (n_tb, further_s)):
        n = ids.shape[1]
        pick_s[:, at : at + n] = one_hot(lax.broadcasted_iota(jnp.int32, (n_sb, n), 0) == ids)
        gather_s[at : at + n, :] = one_hot(jnp.broadcast_to(ids, (BLOCK, n)).T == lane[0:n])

    tail = lax.broadcasted_iota(jnp.int32, (HALF - pc, BLOCK), 0)
    tail = jnp.where(tail < 2, 1.0, 0.0)

    def prepare(k, carry):
        for step in range(4):
            b = k * 4 + step
            y = tpts[:, pl.ds(pl.multiple_of(b * BLOCK, BLOCK), BLOCK)] * ROOT
            y_sq[pl.ds(b, 1), :] = 0.5 * jnp.sum(y * y, axis=0, keepdims=True)
            high, low = split(jnp.concatenate([y, tail], axis=0))
            r_tgt[b] = jnp.concatenate([high, low], axis=0)
        return carry

    per_chunk = n_tb // CHUNKS // 4
    for c in range(CHUNKS):
        loads[c].wait()
        lax.fori_loop(c * per_chunk, (c + 1) * per_chunk, prepare, 0)

    zeros = jnp.zeros((HALF - 56, BLOCK), f32)

    def source(t):
        for h in range(shard_blocks):
            b = t * shard_blocks + h
            xs = xbuf[t, :, h * BLOCK : (h + 1) * BLOCK]
            high, low = split(jnp.concatenate([xs, zeros], axis=0))
            both = jnp.concatenate([high, low], axis=0)
            r_src[b] = both
            a_src[b] = both.T

    def pass_on(d):
        t = lax.rem(my_x + d, nx) * 2 + my_c
        arrived(xbuf.at[t], gather_recv.at[t], chip(d))
        relay = remote(xbuf.at[t], xbuf.at[t], relay_send.at[d], gather_recv.at[t], other_core)
        relay.start()
        return relay

    def from_other(d):
        t = lax.rem(my_x + d, nx) * 2 + 1 - my_c
        arrived(xbuf.at[t], gather_recv.at[t], other_core)
        source(t)

    source(me_t)
    from_other(0)
    near_first = order[::-1]
    relays = [pass_on(d) for d in near_first[:-1]]
    for d in near_first[:-1]:
        source(lax.rem(my_x + d, nx) * 2 + my_c)
    relays.append(pass_on(near_first[-1]))
    for d in near_first[:-1]:
        from_other(d)
    source(lax.rem(my_x + near_first[-1], nx) * 2 + my_c)
    from_other(near_first[-1])
    base_copy.wait()

    def far_columns(k, carry):
        for step in range(UNROLL):
            p = k * UNROLL + step
            row = column_lse(a_src[ids_src[0, n_tb + p]], r_tgt[ids_tgt[0, n_tb + p]])
            far[pl.ds(p, 1), :] = jnp.where(n_tb + p < count, row, LOWEST)
        return carry

    repeat(n_extra // UNROLL, far_columns, 0)

    def band(y):
        return pl.ds(pl.multiple_of(y * per_y, per_y), per_y)

    def to_y(d):
        y = lax.rem(my_y + d, ny)
        return remote(part.at[band(y)], recv_y.at[my_y], y_send.at[d], y_recv.at[my_y], along_y(d))

    def near_columns(ds):
        bands = [lax.rem(my_y + d, ny) for d in ds]
        for y in bands:
            for step in range(per_y):
                b = y * per_y + step
                lse[pl.ds(b, 1), :] = column_lse(a_src[row_ids[0, b]], r_tgt[b])
        for y in bands:
            part[band(y), :] = merge(jnp.stack([lse[band(y), :], extra[band(y), :]]))
        for d in ds:
            if not (isinstance(d, int) and d == 0):
                to_y(d).start()

    extra[...] = owner_steps(far[...], pick_t, gather_t)
    for m in range(ny // 2 - 1):
        near_columns([ny // 2 - m, ny // 2 + 1 + m])
    near_columns([1])
    near_columns([0])
    recv_y[my_y] = part[band(my_y), :]

    def collect(n, me, where, dst, send, recv):
        for d in range(1, n):
            other = lax.rem(me + d, n)
            remote(dst(other), dst(other), send.at[d], recv.at[other], where(d)).wait_recv()

    collect(ny, my_y, along_y, lambda y: recv_y.at[y], y_send, y_recv)
    comb[...] = merge(recv_y[...])

    def to_z(d):
        return remote(comb, recv_z.at[my_z], z_send.at[d], z_recv.at[my_z], along_z(d))

    def by_distance(n):
        return sorted(range(1, n), key=lambda d: -min(d, n - d))

    for d in by_distance(nz):
        to_z(d).start()
    recv_z[my_z] = comb[...]
    collect(nz, my_z, along_z, lambda z: recv_z.at[z], z_send, z_recv)
    full[band(my_y), :] = merge(recv_z[...])

    def to_all(d):
        rows = full.at[band(my_y)]
        return remote(rows, rows, g_send.at[d], g_recv.at[my_y], along_y(d))

    for d in by_distance(ny):
        to_all(d).start()

    line = lax.broadcasted_iota(jnp.int32, (16, BLOCK), 0)

    def near_rows(ds, top):
        bands = [lax.rem(my_y + d, ny) for d in ds]
        values = []
        for y, d in zip(bands, ds):
            rows = band(y)
            if not (isinstance(d, int) and d == 0):
                slot = full.at[rows]
                remote(slot, slot, g_send.at[d], g_recv.at[y], along_y(d)).wait_recv()
        for y in bands:
            rows = band(y)
            total = full[rows, :]
            weight = tlogw[rows, :]
            v = LOG2E * weight - total
            high, low = split(v)
            values.append((high.astype(f32), low.astype(f32), residue(v)))
        for y, (v_high, v_low, rest) in zip(bands, values):
            for step in range(per_y):
                b = y * per_y + step
                r = r_tgt[b]
                one = slice(step, step + 1)
                high = jnp.where(line == 5, rest[one], r[48:64].astype(f32))
                high = jnp.where(line == 4, v_high[one], high)
                low = jnp.where(line == 4, v_low[one], r[112:128].astype(f32))
                both = [r[:48], high.astype(bf16), r[64:112], low.astype(bf16)]
                turned = jnp.concatenate(both, axis=0).T
                a_tgt[b] = turned
                row = column_lse(turned, r_src[row_ids[0, b]])
                lse[pl.ds(b, 1), :] = row
                top = raise_peaks(top, [row], [row_ids[0, b]])
        return top

    row_peak = near_rows([0], jnp.full((n_sb, BLOCK), LOWEST, f32))
    arrivals = sorted(range(1, ny), key=lambda d: min(d, ny - d))
    for group in (arrivals[0:2], arrivals[2:6], arrivals[6:]):
        if group:
            row_peak = near_rows(group, row_peak)

    def far_rows(k, top):
        for step in range(UNROLL):
            p = k * UNROLL + step
            owner = ids_src[0, n_tb + p]
            row = column_lse(a_tgt[ids_tgt[0, n_tb + p]], r_src[owner])
            row = jnp.where(n_tb + p < count, row, LOWEST)
            far[pl.ds(p, 1), :] = row
            top = raise_peaks(top, [row], [owner])
        return top

    row_peak = repeat(n_extra // UNROLL, far_rows, row_peak)
    both = jnp.concatenate([lse[...], far[...]], axis=0)
    rowpart[...] = owner_sums(row_peak, both, pick_s, gather_s)

    def to_t(d):
        return remote(rowpart, recv_x.at[me_t], x_send.at[d], x_recv.at[me_t], along_t(d))

    for d in by_distance(nt):
        to_t(d).start()
    recv_x[me_t] = rowpart[...]
    potential = jnp.concatenate(
        [
            xbuf[t, ROW_F : ROW_F + 1, h * BLOCK : (h + 1) * BLOCK]
            for t in range(nt)
            for h in range(shard_blocks)
        ],
        axis=0,
    )
    rest = potential + 0.5 * slogw[...]
    out_t[...] = 0.5 * tlogw[...] - (0.5 * LN2) * (full[...] - y_sq[...])
    for copy in sent + relays:
        copy.wait_send()
    for n, to in ((ny, to_y), (nz, to_z), (ny, to_all), (nt, to_t)):
        for d in range(1, n):
            to(d).wait_send()
    collect(nt, me_t, along_t, lambda t: recv_x.at[t], x_send, x_recv)
    out_s[...] = rest - (0.5 * LN2) * merge(recv_x[...])


def local(
    n_src,
    n_tgt,
    source_points,
    source_potential,
    source_logw,
    target_points,
    target_logw,
    pair_source,
    pair_target,
    pair_count,
):
    pc, cells = source_points.shape
    n_tb = target_points.shape[1] // BLOCK
    n_sb = source_logw.shape[0] // BLOCK
    slots = pair_source.shape[-1]
    ny = math.isqrt(n_src)
    nz = n_src // ny
    nt = n_tgt
    per_y = n_tb // ny
    n_extra = slots - n_tb
    vmem = pl.BlockSpec(memory_space=pltpu.VMEM)
    dma = pltpu.SemaphoreType.DMA
    out_t, out_s = pl.pallas_call(
        functools.partial(kernel, (ny, nz, nt, n_tb, n_sb, slots, pc)),
        out_shape=(
            pltpu.VMEM((n_tb, BLOCK), f32),
            pltpu.VMEM((n_sb, BLOCK), f32),
        ),
        in_specs=[pl.BlockSpec(memory_space=pltpu.HBM)] * 8,
        out_specs=(vmem, vmem),
        scratch_shapes=[
            pltpu.VMEM((pc, cells), f32),
            pltpu.VMEM((1, cells), f32),
            pltpu.VMEM((n_sb, BLOCK), f32),
            pltpu.VMEM((n_tb, BLOCK), f32),
            pltpu.SMEM((1, slots), jnp.int32),
            pltpu.SMEM((1, slots), jnp.int32),
            pltpu.SMEM((1, 1), jnp.int32),
            pltpu.VMEM((1, slots), jnp.int32),
            pltpu.VMEM((1, slots), jnp.int32),
            pltpu.VMEM((1, slots), jnp.int32),
            pltpu.SMEM((1, slots), jnp.int32),
            pltpu.VMEM((pc, n_tb * BLOCK), f32),
            pltpu.VMEM((nt, 56, cells), f32),
            pltpu.VMEM((n_tb, BLOCK, BLOCK), bf16),
            pltpu.VMEM((n_tb, BLOCK, BLOCK), bf16),
            pltpu.VMEM((n_sb, BLOCK, BLOCK), bf16),
            pltpu.VMEM((n_sb, BLOCK, BLOCK), bf16),
            pltpu.VMEM((n_tb, BLOCK), f32),
            pltpu.VMEM((n_tb, BLOCK), f32),
            pltpu.VMEM((n_extra, BLOCK), f32),
            pltpu.VMEM((n_tb, n_extra), bf16),
            pltpu.VMEM((n_extra, n_tb), bf16),
            pltpu.VMEM((n_sb, slots), bf16),
            pltpu.VMEM((slots, BLOCK), bf16),
            pltpu.VMEM((n_tb, BLOCK), f32),
            pltpu.VMEM((n_tb, BLOCK), f32),
            pltpu.VMEM((ny, per_y, BLOCK), f32),
            pltpu.VMEM((per_y, BLOCK), f32),
            pltpu.VMEM((nz, per_y, BLOCK), f32),
            pltpu.VMEM((n_tb, BLOCK), f32),
            pltpu.VMEM((n_sb, BLOCK), f32),
            pltpu.VMEM((nt, n_sb, BLOCK), f32),
            dma((9,)),
            dma((CHUNKS,)),
            dma,
            dma((nt,)), dma((nt,)), dma((nt,)),
            dma((ny,)), dma((ny,)),
            dma((nz,)), dma((nz,)),
            dma((ny,)), dma((ny,)),
            dma((nt,)), dma((nt,)),
        ],
        compiler_params=pltpu.CompilerParams(
            collective_id=0, has_side_effects=True, vmem_limit_bytes=40 * 2**20
        ),
    )(
        *(
            pltpu.with_memory_space_constraint(operand, pltpu.HBM)
            for operand in (
                source_points,
                source_potential.reshape(1, cells),
                source_logw.reshape(n_sb, BLOCK),
                target_points,
                target_logw.reshape(n_tb, BLOCK),
                pair_source,
                pair_target,
            )
        ),
        pair_count,
    )
    return out_t.reshape(-1), out_s.reshape(-1)


def solution(mesh):
    placed = (
        P(None, ("src", "tgt")),
        P(("src", "tgt")),
        P("src"),
        P(None, "tgt"),
        P("tgt"),
        P("src", "tgt", None),
        P("src", "tgt", None),
        P("src", "tgt"),
    )
    return jax.shard_map(
        functools.partial(local, mesh.shape["src"], mesh.shape["tgt"]),
        mesh=mesh,
        in_specs=placed,
        out_specs=(P("tgt"), P("src")),
        check_vma=False,
    )
```
